512 devices in a mesh: tm: 16 (over x, z_lo, core), patch: 32 (over y, z_hi).
Axes of the slice: x: 4, y: 8, z: 8 (z_hi: 4, z_lo: 2; z = z_hi * 2 + z_lo), core: 2. Of those that a mesh axis runs over, the one named last changes fastest.
Arguments:
- multiplier: float32 [16, 2, 16, 1024, 128], P('tm', None, None, 'patch'), may hold values from -6 to 6
- obs_multiplier: float32 [16, 32768], P('tm', 'patch'), may hold values from -6 to 6
- increment: float32 [16, 2, 16, 1024, 128], P('tm', None, None, 'patch'), may hold values from -6 to 6
- error_var: float32 [16, 2, 16, 1024, 128], P('tm', None, None, 'patch'), may hold values from 0.25 to 4
- obs_var: float32 [16, 32768], P('tm', 'patch'), may hold values from 0.5 to 2
- div_damping: float32 [16, 2, 16, 1024, 128], P('tm', None, None, 'patch'), may hold values from 0.02 to 0.1
- bih_damping: float32 [16, 2, 16, 1024, 128], P('tm', None, None, 'patch'), may hold values from 0.002 to 0.012
- obs_weight: float32 [16, 2, 16, 32768], P('tm', None, None, 'patch'), may hold values from -1 to 1
- obs_cell: int32 [16, 32768], P('tm', 'patch'), may hold values from 0 to 4095
- edge_map: int32 [32, 128], P('patch'), may hold values from 0 to 127, each once within a row
Outputs:
- model_part: float32 [16, 2, 16, 1024, 128], P('tm', None, None, 'patch')
- obs_part: float32 [16, 32768], P('tm', 'patch')
- state_part: float32 [16, 2, 16, 1024, 128], P('tm', None, None, 'patch')
The draws below stay inside these ranges and needn't reach their ends.
Inputs may be any that keep to these rules, and one draw needn't show every extreme that they name: `edge_map`: row p lists, for each column of patch p's first row, the column of patch p-1's last row that lies beside it. `obs_cell`: a cell of the observation's own patch, counted as row * 128 + column within the patch.
All inputs are finite; a program needn't handle non-finite values.
Results may differ from the reference program's by a relative error of at most 0.00002.
Values sent between devices are 32-bit elements; how exact they have to be, the bound alone decides.
A program may use at most 64 MiB of HBM per device.

```python
import math
import jax
import jax.numpy as jnp

LEV = 16
CC = 128
CR = 32
NOBS = 1024
STEPS = 2
SUBWIN = 16
PATCHES = 32
ROWS = 1024
NOBS_ALL = 32768


def with_ends(result, stream_key, smallest, high):
    dims = result.shape
    spot = [jax.random.randint(jax.random.fold_in(stream_key, axis), (), 0, dims[axis]) for axis in range(len(dims))]
    result = result.at[tuple(spot)].set(smallest)
    longest = dims.index(max(dims))
    spot[longest] = (spot[longest] + 1) % dims[longest]
    return result.at[tuple(spot)].set(high)


def block_levels(stream_key, extent, shards, low, high):
    def one(dim, blocks):
        draws = jax.random.uniform(jax.random.fold_in(jax.random.fold_in(stream_key, 6), dim), (blocks,), jnp.float32, low / len(shards), high / len(shards))
        return jnp.repeat(jnp.exp(draws), extent[dim] // blocks).reshape((-1,) + (1,) * (len(extent) - dim - 1))

    level = one(*shards[0])
    for cut in shards[1:]:
        level = level * one(*cut)
    return level


def gaussian(stream_key, shape, scale, reach, shards=(), kind=jnp.bfloat16):
    level = block_levels(stream_key, shape, shards, -0.22, 0.18) if shards else 1.0
    array = jax.random.normal(stream_key, shape, jnp.float32) * scale * level
    return jnp.minimum(jnp.maximum(array, -reach), reach).astype(kind)


def setup_inputs(seed: int = 0) -> dict:
    key_list = jax.random.split(jax.random.key(seed), 11)
    return {
        "multiplier": gaussian(key_list[0], (SUBWIN, 2, LEV, ROWS, CC), 1.0, 6.0, ((0, 16), (3, 32)), jnp.float32),
        "obs_multiplier": gaussian(key_list[1], (SUBWIN, NOBS_ALL), 1.0, 6.0, ((0, 16), (1, 32)), jnp.float32),
        "increment": gaussian(key_list[2], (SUBWIN, 2, LEV, ROWS, CC), 1.0, 6.0, ((0, 16), (3, 32)), jnp.float32),
        "error_var": jnp.clip(jnp.exp(math.log(4.0) - 2.7725887 * jax.random.uniform(key_list[3], (SUBWIN, 2, LEV, ROWS, CC), jnp.float32) ** block_levels(key_list[3], (SUBWIN, 2, LEV, ROWS, CC), ((0, 16), (3, 32)), -0.2, 0.2)), 0.25, 4.0),
        "obs_var": jnp.clip(jnp.exp(math.log(2.0) - 1.3862944 * jax.random.uniform(key_list[4], (SUBWIN, NOBS_ALL), jnp.float32) ** block_levels(key_list[4], (SUBWIN, NOBS_ALL), ((0, 16), (1, 32)), -0.2, 0.2)), 0.5, 2.0),
        "div_damping": jnp.clip(jnp.exp(math.log(0.1) - 1.609438 * jax.random.uniform(key_list[5], (SUBWIN, STEPS, LEV, ROWS, CC), jnp.float32) ** block_levels(key_list[5], (SUBWIN, STEPS, LEV, ROWS, CC), ((0, 16), (3, 32)), -0.2, 0.2)), 0.02, 0.1),
        "bih_damping": jnp.clip(jnp.exp(math.log(0.012) - 1.7917594 * jax.random.uniform(key_list[6], (SUBWIN, STEPS, LEV, ROWS, CC), jnp.float32) ** block_levels(key_list[6], (SUBWIN, STEPS, LEV, ROWS, CC), ((0, 16), (3, 32)), -0.2, 0.2)), 0.002, 0.012),
        "obs_weight": gaussian(key_list[7], (SUBWIN, 2, LEV, NOBS_ALL), (2 * LEV) ** -0.5, 1.0, ((0, 16), (3, 32)), jnp.float32),
        "obs_cell": with_ends(jax.random.randint(key_list[8], (SUBWIN, NOBS_ALL), 0, CR * CC), jax.random.fold_in(key_list[8], 1), 0, (CR * CC) - 1).astype(jnp.int32),
        "edge_map": jax.vmap(lambda own: jax.random.permutation(own, CC))(jax.random.split(key_list[9], PATCHES)).reshape((PATCHES, CC)).astype(jnp.int32),
    }


def column_diff(field):
    return jnp.concatenate([field[..., 1:] - field[..., :-1], jnp.zeros_like(field[..., :1])], -1)


def column_adjoint(field):
    shifted = jnp.concatenate([jnp.zeros_like(field[..., :1]), field[..., :-1]], -1)
    kept = jnp.concatenate([field[..., :-1], jnp.zeros_like(field[..., :1])], -1)
    return shifted - kept


def rows_around(field, inverse, edge_map):
    patch_ids = jnp.arange(PATCHES)[:, None]
    first_rows = field[..., 0, :]
    top_rows = jnp.roll(first_rows[..., patch_ids, inverse], -1, axis=-2)
    last_rows = jnp.roll(field[..., -1, :], 1, axis=-2)
    bottom_rows = last_rows[..., patch_ids, edge_map]
    above_rows = jnp.concatenate([field[..., 1:, :], top_rows[..., None, :]], -2)
    below_rows = jnp.concatenate([bottom_rows[..., None, :], field[..., :-1, :]], -2)
    return above_rows, below_rows


def laplacian(field, above_rows, below_rows):
    return above_rows + below_rows - 2.0 * field - column_adjoint(column_diff(field))


def damp_step(state, div_coef, bih_coef, inverse, edge_map):
    above_rows, below_rows = rows_around(state, inverse, edge_map)
    first_var = state[:, 0]
    second_var = state[:, 1]
    divergence = (above_rows[:, 0] - first_var) + column_diff(second_var)
    scaled_div = div_coef * divergence
    scaled_lap = bih_coef[:, None] * laplacian(state, above_rows, below_rows)
    lap_above, lap_below = rows_around(scaled_lap, inverse, edge_map)
    lap_lap = laplacian(scaled_lap, lap_above, lap_below)
    div_above, div_below = rows_around(scaled_div, inverse, edge_map)
    first_grad = div_below - scaled_div
    second_grad = column_adjoint(scaled_div)
    return state - lap_lap - jnp.stack([first_grad, second_grad], 1)


def observe(field, cells, weights):
    return jnp.sum(weights * field[:, :, cells], axis=(0, 1))


def spread_obs(cells, weights, values):
    empty = jnp.zeros((2, LEV, CR * CC), jnp.float32)
    return empty.at[:, :, cells].add(weights * values)


def reference(multiplier, obs_multiplier, increment, error_var, obs_var, div_damping, bih_damping, obs_weight, obs_cell, edge_map):
    shape_six = (SUBWIN, 2, LEV, PATCHES, CR, CC)
    coef_six = (SUBWIN, STEPS, LEV, PATCHES, CR, CC)
    multi6 = multiplier.reshape(shape_six)
    incr6 = increment.reshape(shape_six)
    div6 = div_damping.reshape(coef_six)
    bih6 = bih_damping.reshape(coef_six)
    patch_ids = jnp.arange(PATCHES)[:, None]
    columns = jnp.broadcast_to(jnp.arange(CC, dtype=jnp.int32)[None, :], (PATCHES, CC))
    inverse = jnp.zeros((PATCHES, CC), jnp.int32).at[patch_ids, edge_map].set(columns)
    forward = jnp.concatenate([jnp.zeros_like(incr6[:1]), incr6[:-1]], 0)
    for step_index in range(STEPS):
        forward = damp_step(forward, div6[:, step_index], bih6[:, step_index], inverse, edge_map)
    adjoint = multi6
    for step_index in reversed(range(STEPS)):
        adjoint = damp_step(adjoint, div6[:, step_index], bih6[:, step_index], inverse, edge_map)
    backward = jnp.concatenate([adjoint[1:], jnp.zeros_like(adjoint[:1])], 0)
    flat = jnp.moveaxis(increment.reshape(SUBWIN, 2, LEV, PATCHES, CR * CC), 3, 1)
    cells = obs_cell.reshape(SUBWIN, PATCHES, NOBS)
    weights = jnp.moveaxis(obs_weight.reshape(SUBWIN, 2, LEV, PATCHES, NOBS), 3, 1)
    observed = jax.vmap(jax.vmap(observe))(flat, cells, weights).reshape(SUBWIN, NOBS_ALL)
    values = obs_multiplier.reshape(SUBWIN, PATCHES, NOBS)
    spread = jax.vmap(jax.vmap(spread_obs))(cells, weights, values)
    spread = jnp.moveaxis(spread, 1, 3).reshape(SUBWIN, 2, LEV, ROWS, CC)
    model_part = error_var * multiplier + increment - forward.reshape(multiplier.shape)
    obs_part = obs_var * obs_multiplier + observed
    state_part = multiplier - backward.reshape(multiplier.shape) + spread
    return model_part, obs_part, state_part
```

```python
import functools

import jax
import jax.numpy as jnp
from jax import lax
from jax.experimental import pallas as pl
from jax.experimental.pallas import tpu as pltpu
from jax.sharding import PartitionSpec as P

MESH = pl.DeviceIdType.MESH
HALO = 4
CHUNKS = 4


def dot_nt(a, b):
    return lax.dot_general(a, b, (((1,), (1,)), ((), ())), preferred_element_type=jnp.float32)


def dot_nn(a, b):
    return lax.dot_general(a, b, (((1,), (0,)), ((), ())), preferred_element_type=jnp.float32)


def split(x):
    hi = x.astype(jnp.bfloat16)
    return hi, (x - hi.astype(jnp.float32)).astype(jnp.bfloat16)


def lane_take(tile, index):
    return jnp.take_along_axis(tile, index, axis=1, mode="promise_in_bounds")


def inverse_rows(perm):
    cols = perm.shape[1]
    target = lax.broadcasted_iota(jnp.int32, (cols, cols), 0)
    hot = (jnp.broadcast_to(perm[0:1], (cols, cols)) == target).astype(jnp.float32).astype(jnp.bfloat16)
    source = lax.broadcasted_iota(jnp.int32, perm.shape, 1).astype(jnp.float32).astype(jnp.bfloat16)
    return dot_nt(source, hot).astype(jnp.int32)


class Geometry:
    def __init__(self, rows, cols, perm, inverse, perm_up, inverse_up):
        self.rows, self.total, self.cols = rows, rows + 2 * HALO, cols
        row = lax.broadcasted_iota(jnp.int32, (8, cols), 0)
        lane = lax.broadcasted_iota(jnp.int32, (8, cols), 1)
        self.up_own = jnp.where(row == 7, inverse_up, lane)
        self.up_halo = jnp.where(row == 7, inverse, lane)
        self.down_own = jnp.where(row == 0, perm, lane)
        self.down_halo = jnp.where(row == 0, perm_up, lane)
        lanes = lax.broadcasted_iota(jnp.int32, (self.total, cols), 1)
        self.first = lanes == 0
        self.last = lanes == cols - 1

    def up(self, f):
        g = pltpu.roll(f, self.total - 1, 0)
        r = self.rows
        return jnp.concatenate(
            [g[: r - 8], lane_take(g[r - 8 : r], self.up_own), lane_take(g[r:], self.up_halo)], 0
        )

    def down(self, f):
        g = pltpu.roll(f, 1, 0)
        r = self.rows
        return jnp.concatenate(
            [lane_take(g[:8], self.down_own), g[8:r], lane_take(g[r:], self.down_halo)], 0
        )

    def right(self, f):
        return jnp.where(self.last, f, pltpu.roll(f, self.cols - 1, 1))

    def left(self, f):
        return jnp.where(self.first, f, pltpu.roll(f, 1, 1))

    def column_adjoint(self, f):
        return jnp.where(self.first, 0.0, pltpu.roll(f, 1, 1)) - jnp.where(self.last, 0.0, f)

    def step(self, u, v, a, b):
        up_u = self.up(u)
        right_v = self.right(v)
        lap_u = (up_u + self.down(u)) + (self.right(u) + self.left(u)) - 4.0 * u
        lap_v = (self.up(v) + self.down(v)) + (right_v + self.left(v)) - 4.0 * v
        sdiv = a * ((up_u - u) + (right_v - v))
        su = b * lap_u
        sv = b * lap_v
        lap_su = (self.up(su) + self.down(su)) + (self.right(su) + self.left(su)) - 4.0 * su
        lap_sv = (self.up(sv) + self.down(sv)) + (self.right(sv) + self.left(sv)) - 4.0 * sv
        return u - lap_su - (self.down(sdiv) - sdiv), v - lap_sv - self.column_adjoint(sdiv)


def kernel(
    sizes,
    obsm, obsv, cell, perm, mult_h, inc_h, err_h, div_h, bih_h, w_h,
    model_h, obs_o, state_h,
    mult, inc, err, div, bih, w, prev, bwd, adj, model, state,
    up_s, down_s, inc_up_s, inc_down_s, low_r, high_r, prev_low, prev_high, perm_s, perm_r,
    a_hi, a_lo, wide, hot,
    load_sem, send_sem, recv_sem, store_sem,
):
    levels, rows, cols, count, n_tm, n_patch = sizes
    k, p = lax.axis_index("tm"), lax.axis_index("patch")
    k_next, k_prev = lax.rem(k + 1, n_tm), lax.rem(k + n_tm - 1, n_tm)
    p_next, p_prev = lax.rem(p + 1, n_patch), lax.rem(p + n_patch - 1, n_patch)

    loads = [
        pltpu.make_async_copy(src, dst, load_sem.at[i])
        for i, (src, dst) in enumerate(
            ((mult_h, mult), (div_h, div), (bih_h, bih), (inc_h, inc), (w_h, w), (err_h, err))
        )
    ]
    for load in loads:
        load.start()

    barrier = pltpu.get_barrier_semaphore()
    for peer in ((k, p_next), (k, p_prev), (k_prev, p), (k_next, p), (k_prev, p_next), (k_prev, p_prev)):
        pl.semaphore_signal(barrier, inc=1, device_id=peer, device_id_type=MESH)

    def remote(index, src, dst, peer):
        return pltpu.make_async_remote_copy(
            src_ref=src, dst_ref=dst, send_sem=send_sem.at[index], recv_sem=recv_sem.at[index],
            device_id=peer, device_id_type=MESH,
        )

    perm_s[...] = jnp.broadcast_to(perm[...], perm_s.shape)
    for i, (load, field) in enumerate(zip(loads[:3], (mult, div, bih))):
        load.wait()
        up_s[2 * i : 2 * i + 2] = field[:, :, rows - HALO :, :]
        down_s[2 * i : 2 * i + 2] = field[:, :, :HALO, :]
    pl.semaphore_wait(barrier, 6)
    rims = [
        remote(0, up_s, low_r, (k, p_next)),
        remote(1, down_s, high_r, (k, p_prev)),
        remote(2, perm_s, perm_r, (k, p_prev)),
    ]
    for copy in rims:
        copy.start()
    bulk = remote(3, inc_h, prev, (k_next, p))
    bulk.start()
    loads[3].wait()
    inc_up_s[...] = inc[:, :, rows - HALO :, :]
    inc_down_s[...] = inc[:, :, :HALO, :]
    inc_rims = [
        remote(4, inc_up_s, prev_low, (k_next, p_next)),
        remote(5, inc_down_s, prev_high, (k_next, p_prev)),
    ]
    for copy in inc_rims:
        copy.start()

    half = rows // 2
    cells = cell[...]
    row = cells // cols
    within = (row // half) * cols + cells % cols
    group = row % half
    hot[...] = (
        lax.broadcasted_iota(jnp.int32, (2 * cols, count), 0) == jnp.broadcast_to(within, (2 * cols, count))
    ).astype(jnp.float32).astype(jnp.bfloat16)
    mask = lax.broadcasted_iota(jnp.int32, (half, count), 0) == jnp.broadcast_to(group, (half, count))
    loads[4].wait()
    loads[5].wait()
    times = obsm[...]
    for var in range(2):
        for lev in range(levels):
            at = (var * levels + lev) * half
            weight = w[var * levels + lev : var * levels + lev + 1, :]
            hi, lo = split(jnp.where(mask, jnp.broadcast_to(weight * times, mask.shape), 0.0))
            a_hi[at : at + half] = hi
            a_lo[at : at + half] = lo
            plane = inc[var, lev]
            hi, lo = split(jnp.concatenate([plane[:half], plane[half:]], 1))
            wide[at : at + half, : 2 * cols] = hi
            wide[at : at + half, 2 * cols :] = lo
    block = min(256, count)
    for start in range(0, count, block):
        part = hot[:, start : start + block]
        found = dot_nn(wide[...], jnp.concatenate([part, part], 0))
        found = found.reshape(2 * levels, half, block)
        found = jnp.where(mask[None, :, start : start + block], found, 0.0)
        found = jnp.sum(found.reshape(2 * levels, half // 8, 8, block), 1)
        found = found * w[:, start : start + block][:, None, :]
        found = jnp.sum(jnp.sum(found, 0), 0, keepdims=True)
        span = pl.ds(start, block)
        obs_o[:, span] = obsv[:, span] * obsm[:, span] + found
    spread = dot_nt(a_hi[...], hot[...]) + dot_nt(a_lo[...], hot[...])
    spread = spread.reshape(2, levels, half, 2 * cols)
    state[:, :, :half, :] = mult[:, :, :half, :] + spread[..., :cols]
    state[:, :, half:, :] = mult[:, :, half:, :] + spread[..., cols:]

    for copy in rims:
        copy.wait()
    own = jnp.broadcast_to(perm[...], perm_r.shape)
    above = perm_r[...]
    geo = Geometry(rows, cols, own, inverse_rows(own), above, inverse_rows(above))

    def whole(field, high, low):
        return jnp.concatenate([field, high, low], 0)

    def coefs(lev, s):
        return (
            whole(div[s, lev], high_r[2 + s, lev], low_r[2 + s, lev]),
            whole(bih[s, lev], high_r[4 + s, lev], low_r[4 + s, lev]),
        )

    per = levels // CHUNKS
    back = []
    for chunk in range(CHUNKS):
        def body(i, _, chunk=chunk):
            lev = chunk * per + i
            u = whole(mult[0, lev], high_r[0, lev], low_r[0, lev])
            v = whole(mult[1, lev], high_r[1, lev], low_r[1, lev])
            for s in (1, 0):
                u, v = geo.step(u, v, *coefs(lev, s))
            adj[0, lev] = u[:rows]
            adj[1, lev] = v[:rows]
            return 0

        lax.fori_loop(0, per, body, 0)
        span = pl.ds(chunk * per, per)
        copy = remote(6 + chunk, adj.at[:, span], bwd.at[:, span], (k_prev, p))
        copy.start()
        back.append(copy)

    bulk.wait()
    for copy in inc_rims:
        copy.wait()
    stores = []
    for chunk in range(CHUNKS):
        def body(i, _, chunk=chunk):
            lev = chunk * per + i
            u = whole(prev[0, lev], prev_high[0, lev], prev_low[0, lev])
            v = whole(prev[1, lev], prev_high[1, lev], prev_low[1, lev])
            for s in (0, 1):
                u, v = geo.step(u, v, *coefs(lev, s))
            for var, f in ((0, u), (1, v)):
                forward = jnp.where(k == 0, 0.0, f[:rows])
                model[var, lev] = err[var, lev] * mult[var, lev] + inc[var, lev] - forward
            return 0

        lax.fori_loop(0, per, body, 0)
        span = pl.ds(chunk * per, per)
        copy = pltpu.make_async_copy(model.at[:, span], model_h.at[:, span], store_sem.at[chunk])
        copy.start()
        stores.append(copy)
    for chunk in range(CHUNKS):
        back[chunk].wait()
        span = pl.ds(chunk * per, per)
        state[:, span] = state[:, span] - jnp.where(k == n_tm - 1, 0.0, bwd[:, span])
        copy = pltpu.make_async_copy(state.at[:, span], state_h.at[:, span], store_sem.at[CHUNKS + chunk])
        copy.start()
        stores.append(copy)
    for copy in stores:
        copy.wait()


def solution(mesh):
    n_tm, n_patch = mesh.shape["tm"], mesh.shape["patch"]

    def per_device(mult, obsm, inc, err, obsv, div, bih, w, cell, perm):
        _, _, levels, rows, cols = mult.shape
        count = obsm.shape[1]
        whole = (2, levels, rows, cols)
        rim = (2, levels, HALO, cols)
        f32 = functools.partial(pltpu.VMEM, dtype=jnp.float32)
        scratch = [f32(whole)] * 5 + [f32((2 * levels, count))] + [f32(whole)] * 5
        scratch += [f32((6,) + rim[1:])] * 2 + [f32(rim)] * 2
        scratch += [f32((6,) + rim[1:])] * 2 + [f32(rim)] * 2
        scratch += [pltpu.VMEM((8, cols), jnp.int32)] * 2
        tall = 2 * levels * (rows // 2)
        scratch += [
            pltpu.VMEM((tall, count), jnp.bfloat16),
            pltpu.VMEM((tall, count), jnp.bfloat16),
            pltpu.VMEM((tall, 4 * cols), jnp.bfloat16),
            pltpu.VMEM((2 * cols, count), jnp.bfloat16),
        ]
        scratch += [
            pltpu.SemaphoreType.DMA((6,)),
            pltpu.SemaphoreType.DMA((6 + CHUNKS,)),
            pltpu.SemaphoreType.DMA((6 + CHUNKS,)),
            pltpu.SemaphoreType.DMA((2 * CHUNKS,)),
        ]
        vmem, any_ = pl.BlockSpec(memory_space=pltpu.VMEM), pl.BlockSpec(memory_space=pltpu.HBM)
        model, obs, state = pl.pallas_call(
            functools.partial(kernel, (levels, rows, cols, count, n_tm, n_patch)),
            out_shape=(
                jax.ShapeDtypeStruct(whole, jnp.float32),
                jax.ShapeDtypeStruct((1, count), jnp.float32),
                jax.ShapeDtypeStruct(whole, jnp.float32),
            ),
            in_specs=[vmem] * 4 + [any_] * 6,
            out_specs=(any_, vmem, any_),
            scratch_shapes=scratch,
            compiler_params=pltpu.CompilerParams(
                collective_id=0, has_side_effects=True, vmem_limit_bytes=48 * 1024 * 1024
            ),
        )(
            obsm, obsv, cell, perm, mult.reshape(whole), inc.reshape(whole), err.reshape(whole),
            div.reshape(whole), bih.reshape(whole), w.reshape(2 * levels, count),
        )
        return model[None], obs, state[None]

    field = P("tm", None, None, "patch", None)
    per_obs = P("tm", "patch")
    return jax.shard_map(
        per_device,
        mesh=mesh,
        in_specs=(
            field, per_obs, field, field, per_obs, field, field,
            P("tm", None, None, "patch"), per_obs, P("patch", None),
        ),
        out_specs=(field, per_obs, field),
        check_vma=False,
    )
```

```python
import functools

import jax
import jax.numpy as jnp
from jax import lax
from jax.experimental import pallas as pl
from jax.experimental.pallas import tpu as pltpu
from jax.sharding import PartitionSpec as P

MESH = pl.DeviceIdType.MESH
HALO = 4
CHUNKS = 4


def dot_nt(a, b):
    return lax.dot_general(a, b, (((1,), (1,)), ((), ())), preferred_element_type=jnp.float32)


def dot_nn(a, b):
    return lax.dot_general(a, b, (((1,), (0,)), ((), ())), preferred_element_type=jnp.float32)


def split(x):
    hi = x.astype(jnp.bfloat16)
    return hi, (x - hi.astype(jnp.float32)).astype(jnp.bfloat16)


def inverse_rows(perm):
    cols = perm.shape[1]
    target = lax.broadcasted_iota(jnp.int32, (cols, cols), 0)
    hot = (jnp.broadcast_to(perm[0:1], (cols, cols)) == target).astype(jnp.float32).astype(jnp.bfloat16)
    source = lax.broadcasted_iota(jnp.int32, perm.shape, 1).astype(jnp.float32).astype(jnp.bfloat16)
    return dot_nt(source, hot).astype(jnp.int32)


def lane_take(tile, index):
    return jnp.take_along_axis(tile, index, axis=1, mode="promise_in_bounds")

class Stencil:
    def __init__(self, cols):
        self.cols = cols
        self.row = lax.broadcasted_iota(jnp.int32, (8, cols), 0)
        self.lane = lax.broadcasted_iota(jnp.int32, (8, cols), 1)
        self.first, self.last = self.lane == 0, self.lane == cols - 1
        self.top, self.bottom = self.row == 7, self.row == 0
        self.low_side, self.high_side = self.row == 3, self.row == 4

    def up(self, tiles):
        r = [pltpu.roll(t, 7, 0) for t in tiles]
        return [jnp.where(self.top, r[(i + 1) % len(r)], r[i]) for i in range(len(r))]

    def down(self, tiles):
        r = [pltpu.roll(t, 1, 0) for t in tiles]
        return [jnp.where(self.bottom, r[i - 1], r[i]) for i in range(len(r))]

    def rows_around(self, tiles, seams):
        above, below = list(tiles), list(tiles)
        for i, index in seams:
            crossed = lane_take(tiles[i], index)
            above[i] = jnp.where(self.high_side, crossed, tiles[i])
            below[i] = jnp.where(self.low_side, crossed, tiles[i])
        return self.up(above), self.down(below)

    def right(self, tiles):
        return [jnp.where(self.last, t, pltpu.roll(t, self.cols - 1, 1)) for t in tiles]

    def left(self, tiles):
        return [jnp.where(self.first, t, pltpu.roll(t, 1, 1)) for t in tiles]

    def lap(self, f, above, below, right):
        return [(a + b) + (r + l) - 4.0 * t for t, a, b, r, l in zip(f, above, below, right, self.left(f))]

    def step(self, u, v, a, b, seams):
        up_u, down_u = self.rows_around(u, seams)
        up_v, down_v = self.rows_around(v, seams)
        right_v = self.right(v)
        sdiv = [c * ((q - p) + (s - r)) for c, p, q, r, s in zip(a, u, up_u, v, right_v)]
        su = [c * t for c, t in zip(b, self.lap(u, up_u, down_u, self.right(u)))]
        sv = [c * t for c, t in zip(b, self.lap(v, up_v, down_v, right_v))]
        lap_su = self.lap(su, *self.rows_around(su, seams), self.right(su))
        lap_sv = self.lap(sv, *self.rows_around(sv, seams), self.right(sv))
        below = self.rows_around(sdiv, seams)[1]
        out_u = [t - l - (q - d) for t, l, q, d in zip(u, lap_su, below, sdiv)]
        out_v = [
            t - l - (jnp.where(self.first, 0.0, pltpu.roll(d, 1, 1)) - jnp.where(self.last, 0.0, d))
            for t, l, d in zip(v, lap_sv, sdiv)
        ]
        return out_u, out_v

    def shift(self, x, y):
        return jnp.where(self.row < 4, pltpu.roll(x, 4, 0), pltpu.roll(y, 4, 0))


def kernel(
    sizes,
    obsm, obsv, cell, perm, mult_h, inc_h, err_h, div_h, bih_h, w_h,
    model_h, obs_o, state_h,
    model, state, mult, inc, err, div, bih, w, prev,
    adj_in, adj_ed, bwd_in, bwd_ed,
    up_s, down_s, inc_up_s, inc_down_s, low_r, high_r, prev_low, prev_high, perm_s, perm_r,
    a_hi, a_lo, wide, hot,
    load_sem, send_sem, recv_sem, store_sem, note_sem,
):
    levels, rows, cols, count, n_tm, n_patch = sizes
    per = levels // CHUNKS
    k, p = lax.axis_index("tm"), lax.axis_index("patch")
    k_next, k_prev = lax.rem(k + 1, n_tm), lax.rem(k + n_tm - 1, n_tm)
    p_next, p_prev = lax.rem(p + 1, n_patch), lax.rem(p + n_patch - 1, n_patch)
    even = lax.rem(p, 2) == 0
    odd = lax.rem(p, 2) == 1
    first = lax.rem(p, 4) == 0
    later = lax.rem(p, 4) != 0

    loads = [
        pltpu.make_async_copy(src, dst, load_sem.at[i])
        for i, (src, dst) in enumerate(
            ((mult_h, mult), (div_h, div), (bih_h, bih), (inc_h, inc), (w_h, w), (err_h, err))
        )
    ]
    for load in loads:
        load.start()

    def remote(index, src, dst, peer):
        return pltpu.make_async_remote_copy(
            src_ref=src, dst_ref=dst, send_sem=send_sem.at[index], recv_sem=recv_sem.at[index],
            device_id=peer, device_id_type=MESH,
        )

    def note(index, peer):
        pl.semaphore_signal(note_sem.at[index], inc=1, device_id=peer, device_id_type=MESH)

    RIM_UP, RIM_DOWN, BACK_IN, BACK_ED, BULK, INC_UP, INC_DOWN, PERM = (i * CHUNKS for i in range(8))
    FROM_ABOVE, FROM_BELOW, BESIDE_ABOVE, BESIDE_BELOW, GO_ABOVE, GO_BELOW = range(6)

    def rim_up(c):
        return remote(RIM_UP + c, up_s.at[c], low_r.at[c], (k, p_next))

    def rim_down(c):
        return remote(RIM_DOWN + c, down_s.at[c], high_r.at[c], (k, p_prev))

    def back_in(c):
        span = pl.ds(c * per, per)
        return remote(BACK_IN + c, adj_in.at[:, span], bwd_in.at[:, span], (k_prev, p))

    def back_ed(c):
        span = pl.ds(c * per, per)
        return remote(BACK_ED + c, adj_ed.at[:, span], bwd_ed.at[:, span], (k_prev, p))

    send_perm = remote(PERM, perm_s, perm_r, (k, p_prev))

    def bulk(c):
        span = pl.ds(c * per, per)
        return remote(BULK + c, inc_h.at[:, span], prev.at[:, span], (k_next, p))

    def inc_up(c):
        return remote(INC_UP + c, inc_up_s.at[c], prev_low.at[c], (k_next, p_next))

    def inc_down(c):
        return remote(INC_DOWN + c, inc_down_s.at[c], prev_high.at[c], (k_next, p_prev))

    def start_all(*copies):
        for copy in copies:
            for c in range(CHUNKS):
                copy(c).start()

    barrier = pltpu.get_barrier_semaphore()

    @pl.when(even)
    def _():
        for peer in ((k_prev, p), (k_next, p), (k, p_prev), (k, p_next)):
            pl.semaphore_signal(barrier, inc=1, device_id=peer, device_id_type=MESH)

    pl.semaphore_wait(barrier, 2)

    @pl.when(odd)
    def _():
        note(FROM_ABOVE, (k, p_prev))
        note(FROM_BELOW, (k, p_next))

    @pl.when(even)
    def _():
        start_all(bulk)

    st = Stencil(cols)
    perm_s[...] = jnp.broadcast_to(perm[...], perm_s.shape)
    for load in loads[:3]:
        load.wait()

    def pack(c, _):
        span = pl.ds(c * per, per)
        for var in range(2):
            up_s[c, var] = mult[var, span, rows - HALO :, :]
            down_s[c, var] = mult[var, span, :HALO, :]
        for i, coef in enumerate((div.at[0], div.at[1], bih.at[0])):
            up_s[c, 2 + i, :, 1:, :] = coef[span, rows - 3 :, :]
            up_s[c, 2 + i, :, :1, :] = bih[1, span, rows - 3 + i : rows - 2 + i, :]
            down_s[c, 2 + i, :, :3, :] = coef[span, :3, :]
            down_s[c, 2 + i, :, 3:, :] = bih[1, span, i : i + 1, :]
        return 0

    lax.fori_loop(0, CHUNKS, pack, 0)

    def send_up():
        start_all(rim_up)

    def send_down():
        send_perm.start()
        start_all(rim_down)

    @pl.when(odd)
    def _():
        send_up()
        send_down()

    loads[3].wait()

    def pack_inc(c, _):
        span = pl.ds(c * per, per)
        inc_up_s[c] = inc[:, span, rows - HALO :, :]
        inc_down_s[c] = inc[:, span, :HALO, :]
        return 0

    lax.fori_loop(0, CHUNKS, pack_inc, 0)

    def inner(field, lev):
        return [field[lev, HALO + 8 * i : HALO + 8 * (i + 1), :] for i in range(rows // 8 - 1)]

    def adjoint_inside(c, _):
        for g in range(per):
            lev = c * per + g
            u, v = inner(mult.at[0], lev), inner(mult.at[1], lev)
            for s in (1, 0):
                u, v = st.step(u, v, inner(div.at[s], lev), inner(bih.at[s], lev), ())
            for var, f in ((0, u), (1, v)):
                for i in range(rows // 8 - 2):
                    adj_in[var, lev, 8 * i : 8 * (i + 1), :] = st.shift(f[i], f[i + 1])

        @pl.when(even)
        def _():
            back_in(c).start()

        return 0

    @pl.when(first)
    def _():
        lax.fori_loop(0, CHUNKS, adjoint_inside, 0)

    @pl.when(even)
    def _():
        pl.semaphore_wait(note_sem.at[FROM_ABOVE], 1)
        send_up()
        note(BESIDE_ABOVE, (k_prev, p))
        note(BESIDE_ABOVE, (k_next, p))
        pl.semaphore_wait(note_sem.at[FROM_BELOW], 1)
        send_down()
        note(BESIDE_BELOW, (k_prev, p))
        note(BESIDE_BELOW, (k_next, p))
        pl.semaphore_wait(note_sem.at[BESIDE_ABOVE], 2)
        note(GO_BELOW, (k, p_next))
        start_all(inc_up)
        pl.semaphore_wait(note_sem.at[BESIDE_BELOW], 2)
        note(GO_ABOVE, (k, p_prev))
        start_all(inc_down)

    @pl.when(odd)
    def _():
        pl.semaphore_wait(note_sem.at[GO_BELOW], 1)
        pl.semaphore_wait(note_sem.at[GO_ABOVE], 1)
        start_all(inc_up, inc_down)

    @pl.when(later)
    def _():
        lax.fori_loop(0, CHUNKS, adjoint_inside, 0)

    half = rows // 2
    cells = cell[...]
    row = cells // cols
    within = (row // half) * cols + cells % cols
    group = row % half
    hot[...] = (
        lax.broadcasted_iota(jnp.int32, (2 * cols, count), 0) == jnp.broadcast_to(within, (2 * cols, count))
    ).astype(jnp.float32).astype(jnp.bfloat16)
    mask = lax.broadcasted_iota(jnp.int32, (half, count), 0) == jnp.broadcast_to(group, (half, count))
    loads[4].wait()
    loads[5].wait()
    times = obsm[...]
    for var in range(2):
        for lev in range(levels):
            at = (var * levels + lev) * half
            weight = w[var * levels + lev : var * levels + lev + 1, :]
            hi, lo = split(jnp.where(mask, jnp.broadcast_to(weight * times, mask.shape), 0.0))
            a_hi[at : at + half] = hi
            a_lo[at : at + half] = lo
            plane = inc[var, lev]
            hi, lo = split(jnp.concatenate([plane[:half], plane[half:]], 1))
            wide[at : at + half, : 2 * cols] = hi
            wide[at : at + half, 2 * cols :] = lo
    block = min(256, count)
    for start in range(0, count, block):
        part = hot[:, start : start + block]
        found = dot_nn(wide[...], jnp.concatenate([part, part], 0))
        found = found.reshape(2 * levels, half, block)
        found = jnp.where(mask[None, :, start : start + block], found, 0.0)
        found = jnp.sum(found.reshape(2 * levels, half // 8, 8, block), 1)
        found = found * w[:, start : start + block][:, None, :]
        found = jnp.sum(jnp.sum(found, 0), 0, keepdims=True)
        span = pl.ds(start, block)
        obs_o[:, span] = obsv[:, span] * obsm[:, span] + found
    spread = dot_nt(a_hi[...], hot[...]) + dot_nt(a_lo[...], hot[...])
    spread = spread.reshape(2, levels, half, 2 * cols)
    state[:, :, :half, :] = mult[:, :, :half, :] + spread[..., :cols]
    state[:, :, half:, :] = mult[:, :, half:, :] + spread[..., cols:]

    @pl.when(odd)
    def _():
        start_all(bulk)

    def keep(var, lev, at, f):
        span = slice(at, at + 8)
        rest = err[var, lev, span, :] * mult[var, lev, span, :] + inc[var, lev, span, :]
        model[var, lev, span, :] = rest - jnp.where(k == 0, 0.0, f)

    def forward_inside(c, _):
        bulk(c).wait_recv()
        for g in range(per):
            lev = c * per + g
            u, v = inner(prev.at[0], lev), inner(prev.at[1], lev)
            for s in (0, 1):
                u, v = st.step(u, v, inner(div.at[s], lev), inner(bih.at[s], lev), ())
            for var, f in ((0, u), (1, v)):
                for i in range(rows // 8 - 2):
                    keep(var, lev, 8 * (i + 1), st.shift(f[i], f[i + 1]))
        return 0

    def all_forward_inside():
        lax.fori_loop(0, CHUNKS, forward_inside, 0)

    @pl.when(even)
    def _():
        all_forward_inside()

    def border(field, high, low, lev):
        return [
            field[lev, rows - 12 : rows - 4, :],
            jnp.concatenate([field[lev, rows - 4 :, :], high], 0),
            jnp.concatenate([low, field[lev, :4, :]], 0),
            field[lev, 4:12, :],
        ]

    def coefs(c, g, s):
        lev = c * per + g
        a = border(div.at[s], high_r[c, 2 + s, g], low_r[c, 2 + s, g], lev)
        if s == 0:
            high, low = high_r[c, 4, g], low_r[c, 4, g]
        else:
            high = jnp.concatenate([high_r[c, 2 + min(i, 2), g, 3:, :] for i in range(4)], 0)
            low = jnp.concatenate([low_r[c, 2 + max(i - 1, 0), g, :1, :] for i in range(4)], 0)
        return a, border(bih.at[s], high, low, lev)

    send_perm.wait_recv()
    own, above = perm_s[...], perm_r[...]

    def seam(low_index, high_index):
        return jnp.where(st.low_side, low_index, jnp.where(st.high_side, high_index, st.lane))

    seams = ((1, seam(above, inverse_rows(above))), (2, seam(own, inverse_rows(own))))

    def adjoint_border(c, _):
        rim_up(c).wait_recv()
        rim_down(c).wait_recv()
        for g in range(per):
            lev = c * per + g
            u, v = (border(mult.at[var], high_r[c, var, g], low_r[c, var, g], lev) for var in range(2))
            for s in (1, 0):
                u, v = st.step(u, v, *coefs(c, g, s), seams)
            for var, f in ((0, u), (1, v)):
                adj_ed[var, lev, :8, :] = st.shift(f[0], f[1])
                adj_ed[var, lev, 8:, :] = st.shift(f[2], f[3])

        @pl.when(odd)
        def _():
            back_in(c).start()

        back_ed(c).start()
        return 0

    lax.fori_loop(0, CHUNKS, adjoint_border, 0)

    @pl.when(odd)
    def _():
        all_forward_inside()

    def model_out(c):
        span = pl.ds(c * per, per)
        return pltpu.make_async_copy(model.at[:, span], model_h.at[:, span], store_sem.at[c])

    def state_out(c):
        span = pl.ds(c * per, per)
        return pltpu.make_async_copy(state.at[:, span], state_h.at[:, span], store_sem.at[CHUNKS + c])

    def forward_border(c, _):
        inc_up(c).wait_recv()
        inc_down(c).wait_recv()
        for g in range(per):
            lev = c * per + g
            u, v = (border(prev.at[var], prev_high[c, var, g], prev_low[c, var, g], lev) for var in range(2))
            for s in (0, 1):
                u, v = st.step(u, v, *coefs(c, g, s), seams)
            for var, f in ((0, u), (1, v)):
                keep(var, lev, rows - 8, st.shift(f[0], f[1]))
                keep(var, lev, 0, st.shift(f[2], f[3]))
        model_out(c).start()
        return 0

    lax.fori_loop(0, CHUNKS, forward_border, 0)
    is_last = k == n_tm - 1

    def finish(c, _):
        span = pl.ds(c * per, per)
        back_in(c).wait_recv()
        inside = pl.ds(8, rows - 16)
        state[:, span, inside, :] = state[:, span, inside, :] - jnp.where(is_last, 0.0, bwd_in[:, span])
        back_ed(c).wait_recv()
        for at, place in ((rows - 8, 0), (0, 8)):
            part = bwd_ed[:, span, place : place + 8, :]
            state[:, span, at : at + 8, :] = state[:, span, at : at + 8, :] - jnp.where(is_last, 0.0, part)
        state_out(c).start()
        return 0

    lax.fori_loop(0, CHUNKS, finish, 0)

    def sent(c, _):
        for copy in (rim_up(c), rim_down(c), back_in(c), back_ed(c), bulk(c), inc_up(c), inc_down(c)):
            copy.wait_send()
        model_out(c).wait()
        state_out(c).wait()
        return 0

    lax.fori_loop(0, CHUNKS, sent, 0)
    send_perm.wait_send()


def hand_over(model_i, obs_i, state_i, model_o, obs_o, state_o, model, obs, state, sems):
    per = model.shape[1] // CHUNKS
    routes = [(obs_i, obs, obs_o)]
    for c in range(CHUNKS):
        span = pl.ds(c * per, per)
        routes.append((model_i.at[:, span], model.at[:, span], model_o.at[:, span]))
        routes.append((state_i.at[:, span], state.at[:, span], state_o.at[:, span]))
    ins = [pltpu.make_async_copy(a, b, sems.at[i]) for i, (a, b, _) in enumerate(routes)]
    outs = [pltpu.make_async_copy(b, c, sems.at[len(routes) + i]) for i, (_, b, c) in enumerate(routes)]
    for copy in ins:
        copy.start()
    for came, goes in zip(ins, outs):
        came.wait()
        goes.start()
    for copy in outs:
        copy.wait()


def solution(mesh):
    n_tm, n_patch = mesh.shape["tm"], mesh.shape["patch"]

    def per_device(mult, obsm, inc, err, obsv, div, bih, w, cell, perm):
        _, _, levels, rows, cols = mult.shape
        count = obsm.shape[1]
        per = levels // CHUNKS
        whole = (2, levels, rows, cols)
        rim = (CHUNKS, 2, per, HALO, cols)
        rims = (CHUNKS, 5, per, HALO, cols)
        f32 = functools.partial(pltpu.VMEM, dtype=jnp.float32)
        scratch = [f32(whole)] * 7 + [f32((2 * levels, count)), f32(whole)]
        scratch += [f32((2, levels, rows - 16, cols)), f32((2, levels, 16, cols))] * 2
        scratch += [f32(rims)] * 2 + [f32(rim)] * 2
        scratch += [f32(rims)] * 2 + [f32(rim)] * 2
        scratch += [pltpu.VMEM((8, cols), jnp.int32)] * 2
        tall = 2 * levels * (rows // 2)
        scratch += [
            pltpu.VMEM((tall, count), jnp.bfloat16),
            pltpu.VMEM((tall, count), jnp.bfloat16),
            pltpu.VMEM((tall, 4 * cols), jnp.bfloat16),
            pltpu.VMEM((2 * cols, count), jnp.bfloat16),
        ]
        copies = 7 * CHUNKS + 1
        scratch += [
            pltpu.SemaphoreType.DMA((6,)),
            pltpu.SemaphoreType.DMA((copies,)),
            pltpu.SemaphoreType.DMA((copies,)),
            pltpu.SemaphoreType.DMA((2 * CHUNKS,)),
            pltpu.SemaphoreType.REGULAR((6,)),
        ]
        vmem, any_ = pl.BlockSpec(memory_space=pltpu.VMEM), pl.BlockSpec(memory_space=pl.ANY)
        shapes = (
            jax.ShapeDtypeStruct(whole, jnp.float32),
            jax.ShapeDtypeStruct((1, count), jnp.float32),
            jax.ShapeDtypeStruct(whole, jnp.float32),
        )
        parts = pl.pallas_call(
            functools.partial(kernel, (levels, rows, cols, count, n_tm, n_patch)),
            out_shape=shapes,
            in_specs=[vmem] * 4 + [any_] * 6,
            out_specs=(any_, vmem, any_),
            scratch_shapes=scratch,
            compiler_params=pltpu.CompilerParams(
                collective_id=0, has_side_effects=True, vmem_limit_bytes=60 * 1024 * 1024
            ),
        )(
            obsm, obsv, cell, perm, mult.reshape(whole), inc.reshape(whole), err.reshape(whole),
            div.reshape(whole), bih.reshape(whole), w.reshape(2 * levels, count),
        )
        model, obs, state = pl.pallas_call(
            hand_over,
            out_shape=shapes,
            in_specs=[any_] * 3,
            out_specs=(any_,) * 3,
            scratch_shapes=[f32(whole), f32((1, count)), f32(whole), pltpu.SemaphoreType.DMA((4 * CHUNKS + 2,))],
            compiler_params=pltpu.CompilerParams(vmem_limit_bytes=60 * 1024 * 1024),
        )(*parts)
        return model[None], obs, state[None]

    field = P("tm", None, None, "patch", None)
    per_obs = P("tm", "patch")
    return jax.shard_map(
        per_device,
        mesh=mesh,
        in_specs=(
            field, per_obs, field, field, per_obs, field, field,
            P("tm", None, None, "patch"), per_obs, P("patch", None),
        ),
        out_specs=(field, per_obs, field),
        check_vma=False,
    )
```

```python
import functools

import jax
import jax.numpy as jnp
from jax import lax
from jax.experimental import pallas as pl
from jax.experimental.pallas import tpu as pltpu
from jax.sharding import PartitionSpec as P

MESH = pl.DeviceIdType.MESH
HALO = 4
CHUNKS = 4


def dot_nt(a, b):
    return lax.dot_general(a, b, (((1,), (1,)), ((), ())), preferred_element_type=jnp.float32)


def dot_nn(a, b):
    return lax.dot_general(a, b, (((1,), (0,)), ((), ())), preferred_element_type=jnp.float32)


def split(x):
    hi = x.astype(jnp.bfloat16)
    return hi, (x - hi.astype(jnp.float32)).astype(jnp.bfloat16)


def inverse_rows(perm):
    cols = perm.shape[1]
    target = lax.broadcasted_iota(jnp.int32, (cols, cols), 0)
    hot = (jnp.broadcast_to(perm[0:1], (cols, cols)) == target).astype(jnp.float32).astype(jnp.bfloat16)
    source = lax.broadcasted_iota(jnp.int32, perm.shape, 1).astype(jnp.float32).astype(jnp.bfloat16)
    return dot_nt(source, hot).astype(jnp.int32)


def lane_take(tile, index):
    return jnp.take_along_axis(tile, index, axis=1, mode="promise_in_bounds")

class Stencil:
    def __init__(self, cols):
        self.cols = cols
        self.row = lax.broadcasted_iota(jnp.int32, (8, cols), 0)
        self.lane = lax.broadcasted_iota(jnp.int32, (8, cols), 1)
        self.first, self.last = self.lane == 0, self.lane == cols - 1
        self.top, self.bottom = self.row == 7, self.row == 0
        self.low_side, self.high_side = self.row == 3, self.row == 4

    def up(self, tiles):
        r = [pltpu.roll(t, 7, 0) for t in tiles]
        return [jnp.where(self.top, r[(i + 1) % len(r)], r[i]) for i in range(len(r))]

    def down(self, tiles):
        r = [pltpu.roll(t, 1, 0) for t in tiles]
        return [jnp.where(self.bottom, r[i - 1], r[i]) for i in range(len(r))]

    def rows_around(self, tiles, seams):
        above, below = list(tiles), list(tiles)
        for i, index in seams:
            crossed = lane_take(tiles[i], index)
            above[i] = jnp.where(self.high_side, crossed, tiles[i])
            below[i] = jnp.where(self.low_side, crossed, tiles[i])
        return self.up(above), self.down(below)

    def right(self, tiles):
        return [jnp.where(self.last, t, pltpu.roll(t, self.cols - 1, 1)) for t in tiles]

    def left(self, tiles):
        return [jnp.where(self.first, t, pltpu.roll(t, 1, 1)) for t in tiles]

    def lap(self, f, above, below, right):
        return [(a + b) + (r + l) - 4.0 * t for t, a, b, r, l in zip(f, above, below, right, self.left(f))]

    def step(self, u, v, a, b, seams):
        up_u, down_u = self.rows_around(u, seams)
        up_v, down_v = self.rows_around(v, seams)
        right_v = self.right(v)
        sdiv = [c * ((q - p) + (s - r)) for c, p, q, r, s in zip(a, u, up_u, v, right_v)]
        su = [c * t for c, t in zip(b, self.lap(u, up_u, down_u, self.right(u)))]
        sv = [c * t for c, t in zip(b, self.lap(v, up_v, down_v, right_v))]
        lap_su = self.lap(su, *self.rows_around(su, seams), self.right(su))
        lap_sv = self.lap(sv, *self.rows_around(sv, seams), self.right(sv))
        below = self.rows_around(sdiv, seams)[1]
        out_u = [t - l - (q - d) for t, l, q, d in zip(u, lap_su, below, sdiv)]
        out_v = [
            t - l - (jnp.where(self.first, 0.0, pltpu.roll(d, 1, 1)) - jnp.where(self.last, 0.0, d))
            for t, l, d in zip(v, lap_sv, sdiv)
        ]
        return out_u, out_v

    def shift(self, x, y):
        return jnp.where(self.row < 4, pltpu.roll(x, 4, 0), pltpu.roll(y, 4, 0))


def kernel(
    sizes,
    obsm, obsv, cell, perm, mult_h, inc_h, err_h, div_h, bih_h, w_h,
    model, obs_o, state,
    mult, inc, err, div, bih, w, prev,
    adj_in, adj_ed, bwd_in, bwd_ed,
    up_s, down_s, inc_up_s, inc_down_s, low_r, high_r, prev_low, prev_high, perm_s, perm_r,
    a_hi, a_lo, wide, hot,
    load_sem, send_sem, recv_sem, store_sem, note_sem,
):
    levels, rows, cols, count, n_tm, n_patch = sizes
    per = levels // CHUNKS
    k, p = lax.axis_index("tm"), lax.axis_index("patch")
    k_next, k_prev = lax.rem(k + 1, n_tm), lax.rem(k + n_tm - 1, n_tm)
    p_next, p_prev = lax.rem(p + 1, n_patch), lax.rem(p + n_patch - 1, n_patch)
    has_next, has_prev = k < n_tm - 1, k > 0
    quad = lax.rem(p, 4)
    early, late = quad < 2, quad >= 2

    loads = [
        pltpu.make_async_copy(src, dst, load_sem.at[i])
        for i, (src, dst) in enumerate(
            ((mult_h, mult), (div_h, div), (bih_h, bih), (inc_h, inc), (w_h, w), (err_h, err))
        )
    ]
    for load in loads:
        load.start()

    def remote(index, src, dst, peer):
        return pltpu.make_async_remote_copy(
            src_ref=src, dst_ref=dst, send_sem=send_sem.at[index], recv_sem=recv_sem.at[index],
            device_id=peer, device_id_type=MESH,
        )

    def note(index, peer):
        pl.semaphore_signal(note_sem.at[index], inc=1, device_id=peer, device_id_type=MESH)

    RIM_UP, RIM_DOWN, BACK_IN, BACK_ED, BULK, INC_UP, INC_DOWN, PERM = (i * CHUNKS for i in range(8))
    FROM_ABOVE, FROM_BELOW, BESIDE_ABOVE, BESIDE_BELOW = range(4)

    def rim_up(c):
        return remote(RIM_UP + c, up_s.at[c], low_r.at[c], (k, p_next))

    def rim_down(c):
        return remote(RIM_DOWN + c, down_s.at[c], high_r.at[c], (k, p_prev))

    def back_in(c):
        span = pl.ds(c * per, per)
        return remote(BACK_IN + c, adj_in.at[:, span], bwd_in.at[:, span], (k_prev, p))

    def back_ed(c):
        span = pl.ds(c * per, per)
        return remote(BACK_ED + c, adj_ed.at[:, span], bwd_ed.at[:, span], (k_prev, p))

    send_perm = remote(PERM, perm_s, perm_r, (k, p_prev))

    def bulk(c):
        span = pl.ds(c * per, per)
        return remote(BULK + c, inc_h.at[:, span], prev.at[:, span], (k_next, p))

    def inc_up(c):
        return remote(INC_UP + c, inc_up_s.at[c], prev_low.at[c], (k_next, p_next))

    def inc_down(c):
        return remote(INC_DOWN + c, inc_down_s.at[c], prev_high.at[c], (k_next, p_prev))

    def start_all(*copies):
        for copy in copies:
            for c in range(CHUNKS):
                copy(c).start()

    def start_next(*copies):
        @pl.when(has_next)
        def _():
            start_all(*copies)

    barrier = pltpu.get_barrier_semaphore()
    for peer in ((k_prev, p), (k_next, p)):
        pl.semaphore_signal(barrier, inc=1, device_id=peer, device_id_type=MESH)

    @pl.when(quad != 3)
    def _():
        pl.semaphore_signal(barrier, inc=1, device_id=(k, p_next), device_id_type=MESH)

    @pl.when(quad == 0)
    def _():
        pl.semaphore_signal(barrier, inc=1, device_id=(k, p_prev), device_id_type=MESH)

    pl.semaphore_wait(barrier, jnp.where(quad == 0, 2, jnp.where(quad == 3, 4, 3)))

    def send_inc_up():
        pl.semaphore_wait(note_sem.at[BESIDE_ABOVE], 1)
        start_next(inc_up)

    def send_inc_down():
        pl.semaphore_wait(note_sem.at[BESIDE_BELOW], 1)
        start_next(inc_down)

    @pl.when(quad != 0)
    def _():
        note(FROM_ABOVE, (k, p_prev))
        note(BESIDE_BELOW, (k_prev, p))

    @pl.when(quad == 3)
    def _():
        note(FROM_BELOW, (k, p_next))
        note(BESIDE_ABOVE, (k_prev, p))

    @pl.when(early)
    def _():
        start_next(bulk)

    st = Stencil(cols)
    perm_s[...] = jnp.broadcast_to(perm[...], perm_s.shape)
    for load in loads[:3]:
        load.wait()

    def pack(c, _):
        span = pl.ds(c * per, per)
        for var in range(2):
            up_s[c, var] = mult[var, span, rows - HALO :, :]
            down_s[c, var] = mult[var, span, :HALO, :]
        for i, coef in enumerate((div.at[0], div.at[1], bih.at[0])):
            up_s[c, 2 + i, :, 1:, :] = coef[span, rows - 3 :, :]
            up_s[c, 2 + i, :, :1, :] = bih[1, span, rows - 3 + i : rows - 2 + i, :]
            down_s[c, 2 + i, :, :3, :] = coef[span, :3, :]
            down_s[c, 2 + i, :, 3:, :] = bih[1, span, i : i + 1, :]
        return 0

    lax.fori_loop(0, CHUNKS, pack, 0)

    def send_up():
        start_all(rim_up)

    def send_down():
        send_perm.start()
        start_all(rim_down)

    def meet_above():
        pl.semaphore_wait(note_sem.at[FROM_ABOVE], 1)
        send_up()
        note(BESIDE_ABOVE, (k_prev, p))

    @pl.when(quad != 0)
    def _():
        send_down()

    @pl.when(quad == 3)
    def _():
        send_up()

    @pl.when(quad == 2)
    def _():
        meet_above()

    loads[3].wait()

    def pack_inc(c, _):
        span = pl.ds(c * per, per)
        inc_up_s[c] = inc[:, span, rows - HALO :, :]
        inc_down_s[c] = inc[:, span, :HALO, :]
        return 0

    lax.fori_loop(0, CHUNKS, pack_inc, 0)

    @pl.when(quad != 0)
    def _():
        send_inc_down()

    @pl.when(late)
    def _():
        send_inc_up()

    def inner(field, lev):
        return [field[lev, HALO + 8 * i : HALO + 8 * (i + 1), :] for i in range(rows // 8 - 1)]

    def adjoint_inside(c, _):
        for g in range(per):
            lev = c * per + g
            u, v = inner(mult.at[0], lev), inner(mult.at[1], lev)
            for s in (1, 0):
                u, v = st.step(u, v, inner(div.at[s], lev), inner(bih.at[s], lev), ())
            for var, f in ((0, u), (1, v)):
                for i in range(rows // 8 - 2):
                    adj_in[var, lev, 8 * i : 8 * (i + 1), :] = st.shift(f[i], f[i + 1])

        @pl.when(early & has_prev)
        def _():
            back_in(c).start()

        return 0

    lax.fori_loop(0, CHUNKS, adjoint_inside, 0)

    @pl.when(early)
    def _():
        meet_above()

    @pl.when(quad == 1)
    def _():
        send_inc_up()

    @pl.when(late)
    def _():
        start_next(bulk)

    half = rows // 2
    cells = cell[...]
    row = cells // cols
    within = (row // half) * cols + cells % cols
    group = row % half
    hot[...] = (
        lax.broadcasted_iota(jnp.int32, (2 * cols, count), 0) == jnp.broadcast_to(within, (2 * cols, count))
    ).astype(jnp.float32).astype(jnp.bfloat16)
    mask = lax.broadcasted_iota(jnp.int32, (half, count), 0) == jnp.broadcast_to(group, (half, count))
    loads[4].wait()
    loads[5].wait()
    times = obsm[...]
    for var in range(2):
        for lev in range(levels):
            at = (var * levels + lev) * half
            weight = w[var * levels + lev : var * levels + lev + 1, :]
            hi, lo = split(jnp.where(mask, jnp.broadcast_to(weight * times, mask.shape), 0.0))
            a_hi[at : at + half] = hi
            a_lo[at : at + half] = lo
            plane = inc[var, lev]
            hi, lo = split(jnp.concatenate([plane[:half], plane[half:]], 1))
            wide[at : at + half, : 2 * cols] = hi
            wide[at : at + half, 2 * cols :] = lo
    block = min(256, count)
    for start in range(0, count, block):
        part = hot[:, start : start + block]
        found = dot_nn(wide[...], jnp.concatenate([part, part], 0))
        found = found.reshape(2 * levels, half, block)
        found = jnp.where(mask[None, :, start : start + block], found, 0.0)
        found = jnp.sum(found.reshape(2 * levels, half // 8, 8, block), 1)
        found = found * w[:, start : start + block][:, None, :]
        found = jnp.sum(jnp.sum(found, 0), 0, keepdims=True)
        span = pl.ds(start, block)
        obs_o[:, span] = obsv[:, span] * obsm[:, span] + found
    spread = dot_nt(a_hi[...], hot[...]) + dot_nt(a_lo[...], hot[...])
    spread = spread.reshape(2, levels, half, 2 * cols)
    state[:, :, :half, :] = mult[:, :, :half, :] + spread[..., :cols]
    state[:, :, half:, :] = mult[:, :, half:, :] + spread[..., cols:]

    @pl.when(quad == 0)
    def _():
        send_inc_up()
        pl.semaphore_wait(note_sem.at[FROM_BELOW], 1)
        send_down()
        note(BESIDE_BELOW, (k_prev, p))
        send_inc_down()

    def keep(var, lev, at, f):
        span = slice(at, at + 8)
        rest = err[var, lev, span, :] * mult[var, lev, span, :] + inc[var, lev, span, :]
        model[var, lev, span, :] = rest - jnp.where(has_prev, f, 0.0)

    def forward_inside(c, _):
        @pl.when(has_prev)
        def _():
            bulk(c).wait_recv()

        for g in range(per):
            lev = c * per + g
            u, v = inner(prev.at[0], lev), inner(prev.at[1], lev)
            for s in (0, 1):
                u, v = st.step(u, v, inner(div.at[s], lev), inner(bih.at[s], lev), ())
            for var, f in ((0, u), (1, v)):
                for i in range(rows // 8 - 2):
                    keep(var, lev, 8 * (i + 1), st.shift(f[i], f[i + 1]))
        return 0

    def all_forward_inside():
        lax.fori_loop(0, CHUNKS, forward_inside, 0)

    @pl.when(early)
    def _():
        all_forward_inside()

    def border(field, high, low, lev):
        return [
            field[lev, rows - 12 : rows - 4, :],
            jnp.concatenate([field[lev, rows - 4 :, :], high], 0),
            jnp.concatenate([low, field[lev, :4, :]], 0),
            field[lev, 4:12, :],
        ]

    def coefs(c, g, s):
        lev = c * per + g
        a = border(div.at[s], high_r[c, 2 + s, g], low_r[c, 2 + s, g], lev)
        if s == 0:
            high, low = high_r[c, 4, g], low_r[c, 4, g]
        else:
            high = jnp.concatenate([high_r[c, 2 + min(i, 2), g, 3:, :] for i in range(4)], 0)
            low = jnp.concatenate([low_r[c, 2 + max(i - 1, 0), g, :1, :] for i in range(4)], 0)
        return a, border(bih.at[s], high, low, lev)

    send_perm.wait_recv()
    own, above = perm_s[...], perm_r[...]

    def seam(low_index, high_index):
        return jnp.where(st.low_side, low_index, jnp.where(st.high_side, high_index, st.lane))

    seams = ((1, seam(above, inverse_rows(above))), (2, seam(own, inverse_rows(own))))

    def adjoint_border(c, _):
        rim_up(c).wait_recv()
        rim_down(c).wait_recv()
        for g in range(per):
            lev = c * per + g
            u, v = (border(mult.at[var], high_r[c, var, g], low_r[c, var, g], lev) for var in range(2))
            for s in (1, 0):
                u, v = st.step(u, v, *coefs(c, g, s), seams)
            for var, f in ((0, u), (1, v)):
                adj_ed[var, lev, :8, :] = st.shift(f[0], f[1])
                adj_ed[var, lev, 8:, :] = st.shift(f[2], f[3])

        @pl.when(late & has_prev)
        def _():
            back_in(c).start()

        @pl.when(has_prev)
        def _():
            back_ed(c).start()

        return 0

    lax.fori_loop(0, CHUNKS, adjoint_border, 0)

    @pl.when(late)
    def _():
        all_forward_inside()

    def model_out(c):
        span = pl.ds(c * per, per)
        return pltpu.make_async_copy(model.at[:, span], model_h.at[:, span], store_sem.at[c])

    def state_out(c):
        span = pl.ds(c * per, per)
        return pltpu.make_async_copy(state.at[:, span], state_h.at[:, span], store_sem.at[CHUNKS + c])

    def forward_border(c, _):
        @pl.when(has_prev)
        def _():
            inc_up(c).wait_recv()
            inc_down(c).wait_recv()

        for g in range(per):
            lev = c * per + g
            u, v = (border(prev.at[var], prev_high[c, var, g], prev_low[c, var, g], lev) for var in range(2))
            for s in (0, 1):
                u, v = st.step(u, v, *coefs(c, g, s), seams)
            for var, f in ((0, u), (1, v)):
                keep(var, lev, rows - 8, st.shift(f[0], f[1]))
                keep(var, lev, 0, st.shift(f[2], f[3]))
        return 0

    lax.fori_loop(0, CHUNKS, forward_border, 0)

    def finish(c, _):
        span = pl.ds(c * per, per)

        @pl.when(has_next)
        def _():
            back_in(c).wait_recv()
            back_ed(c).wait_recv()

        inside = pl.ds(8, rows - 16)
        state[:, span, inside, :] = state[:, span, inside, :] - jnp.where(has_next, bwd_in[:, span], 0.0)
        for at, place in ((rows - 8, 0), (0, 8)):
            part = bwd_ed[:, span, place : place + 8, :]
            state[:, span, at : at + 8, :] = state[:, span, at : at + 8, :] - jnp.where(has_next, part, 0.0)
        return 0

    lax.fori_loop(0, CHUNKS, finish, 0)

    def sent(c, _):
        rim_up(c).wait_send()
        rim_down(c).wait_send()

        @pl.when(has_prev)
        def _():
            back_in(c).wait_send()
            back_ed(c).wait_send()

        @pl.when(has_next)
        def _():
            bulk(c).wait_send()
            inc_up(c).wait_send()
            inc_down(c).wait_send()

        return 0

    lax.fori_loop(0, CHUNKS, sent, 0)
    send_perm.wait_send()


def hand_over(*refs):
    sems = refs[-1]
    copies = [pltpu.make_async_copy(refs[i], refs[3 + i], sems.at[i]) for i in range(3)]
    for copy in copies:
        copy.start()
    for copy in copies:
        copy.wait()


def solution(mesh):
    n_tm, n_patch = mesh.shape["tm"], mesh.shape["patch"]

    def per_device(mult, obsm, inc, err, obsv, div, bih, w, cell, perm):
        _, _, levels, rows, cols = mult.shape
        count = obsm.shape[1]
        per = levels // CHUNKS
        whole = (2, levels, rows, cols)
        rim = (CHUNKS, 2, per, HALO, cols)
        rims = (CHUNKS, 5, per, HALO, cols)
        f32 = functools.partial(pltpu.VMEM, dtype=jnp.float32)
        scratch = [f32(whole)] * 5 + [f32((2 * levels, count)), f32(whole)]
        scratch += [f32((2, levels, rows - 16, cols)), f32((2, levels, 16, cols))] * 2
        scratch += [f32(rims)] * 2 + [f32(rim)] * 2
        scratch += [f32(rims)] * 2 + [f32(rim)] * 2
        scratch += [pltpu.VMEM((8, cols), jnp.int32)] * 2
        tall = 2 * levels * (rows // 2)
        scratch += [
            pltpu.VMEM((tall, count), jnp.bfloat16),
            pltpu.VMEM((tall, count), jnp.bfloat16),
            pltpu.VMEM((tall, 4 * cols), jnp.bfloat16),
            pltpu.VMEM((2 * cols, count), jnp.bfloat16),
        ]
        copies = 7 * CHUNKS + 1
        scratch += [
            pltpu.SemaphoreType.DMA((6,)),
            pltpu.SemaphoreType.DMA((copies,)),
            pltpu.SemaphoreType.DMA((copies,)),
            pltpu.SemaphoreType.DMA((2 * CHUNKS,)),
            pltpu.SemaphoreType.REGULAR((4,)),
        ]
        vmem, any_ = pl.BlockSpec(memory_space=pltpu.VMEM), pl.BlockSpec(memory_space=pl.ANY)
        shapes = (
            jax.ShapeDtypeStruct(whole, jnp.float32),
            jax.ShapeDtypeStruct((1, count), jnp.float32),
            jax.ShapeDtypeStruct(whole, jnp.float32),
        )
        parts = pl.pallas_call(
            functools.partial(kernel, (levels, rows, cols, count, n_tm, n_patch)),
            out_shape=tuple(pltpu.VMEM(x.shape, x.dtype) for x in shapes),
            in_specs=[vmem] * 4 + [any_] * 6,
            out_specs=(vmem, vmem, vmem),
            scratch_shapes=scratch,
            compiler_params=pltpu.CompilerParams(
                collective_id=0, has_side_effects=True, vmem_limit_bytes=62914560
            ),
        )(
            obsm, obsv, cell, perm, mult.reshape(whole), inc.reshape(whole), err.reshape(whole),
            div.reshape(whole), bih.reshape(whole), w.reshape(2 * levels, count),
        )
        model, obs, state = pl.pallas_call(
            hand_over,
            out_shape=shapes,
            in_specs=[vmem] * 3,
            out_specs=(any_,) * 3,
            scratch_shapes=[pltpu.SemaphoreType.DMA((3,))],
            compiler_params=pltpu.CompilerParams(vmem_limit_bytes=16777216),
        )(*parts)
        return model[None], obs, state[None]

    field = P("tm", None, None, "patch", None)
    per_obs = P("tm", "patch")
    return jax.shard_map(
        per_device,
        mesh=mesh,
        in_specs=(
            field, per_obs, field, field, per_obs, field, field,
            P("tm", None, None, "patch"), per_obs, P("patch", None),
        ),
        out_specs=(field, per_obs, field),
        check_vma=False,
    )
```

```python
import functools

import jax
import jax.numpy as jnp
from jax import lax
from jax.experimental import pallas as pl
from jax.experimental.pallas import tpu as pltpu
from jax.sharding import PartitionSpec as P

MESH = pl.DeviceIdType.MESH
CHUNKS = 4


def dot_nt(a, b):
    return lax.dot_general(a, b, (((1,), (1,)), ((), ())), preferred_element_type=jnp.float32)


def dot_nn(a, b):
    return lax.dot_general(a, b, (((1,), (0,)), ((), ())), preferred_element_type=jnp.float32)


def split(x):
    hi = x.astype(jnp.bfloat16)
    return hi, (x - hi.astype(jnp.float32)).astype(jnp.bfloat16)


def inverse_rows(perm):
    cols = perm.shape[1]
    target = lax.broadcasted_iota(jnp.int32, (cols, cols), 0)
    hot = (jnp.broadcast_to(perm[0:1], (cols, cols)) == target).astype(jnp.float32).astype(jnp.bfloat16)
    source = lax.broadcasted_iota(jnp.int32, perm.shape, 1).astype(jnp.float32).astype(jnp.bfloat16)
    return dot_nt(source, hot).astype(jnp.int32)


def lane_take(tile, index):
    return jnp.take_along_axis(tile, index, axis=1, mode="promise_in_bounds")

class Stencil:
    def __init__(self, cols):
        self.cols = cols
        self.row = lax.broadcasted_iota(jnp.int32, (8, cols), 0)
        self.lane = lax.broadcasted_iota(jnp.int32, (8, cols), 1)
        self.first, self.last = self.lane == 0, self.lane == cols - 1
        self.top, self.bottom = self.row == 7, self.row == 0
        self.below_edge = (self.row == 5, self.row == 1)
        self.above_edge = (self.row == 6, self.row == 2)

    def up(self, tiles):
        r = [pltpu.roll(t, 7, 0) for t in tiles]
        return [jnp.where(self.top, r[(i + 1) % len(r)], r[i]) for i in range(len(r))]

    def down(self, tiles):
        r = [pltpu.roll(t, 1, 0) for t in tiles]
        return [jnp.where(self.bottom, r[i - 1], r[i]) for i in range(len(r))]

    def rows_around(self, tiles, seams):
        above, below = list(tiles), list(tiles)
        for i, index in enumerate(seams):
            crossed = lane_take(tiles[i], index)
            above[i] = jnp.where(self.above_edge[i], crossed, tiles[i])
            below[i] = jnp.where(self.below_edge[i], crossed, tiles[i])
        return self.up(above), self.down(below)

    def right(self, tiles):
        return [jnp.where(self.last, t, pltpu.roll(t, self.cols - 1, 1)) for t in tiles]

    def left(self, tiles):
        return [jnp.where(self.first, t, pltpu.roll(t, 1, 1)) for t in tiles]

    def lap(self, f, above, below, right):
        return [(a + b) + (r + l) - 4.0 * t for t, a, b, r, l in zip(f, above, below, right, self.left(f))]

    def step(self, u, v, a, b, seams):
        up_u, down_u = self.rows_around(u, seams)
        up_v, down_v = self.rows_around(v, seams)
        right_v = self.right(v)
        sdiv = [c * ((q - p) + (s - r)) for c, p, q, r, s in zip(a, u, up_u, v, right_v)]
        su = [c * t for c, t in zip(b, self.lap(u, up_u, down_u, self.right(u)))]
        sv = [c * t for c, t in zip(b, self.lap(v, up_v, down_v, right_v))]
        lap_su = self.lap(su, *self.rows_around(su, seams), self.right(su))
        lap_sv = self.lap(sv, *self.rows_around(sv, seams), self.right(sv))
        below = self.rows_around(sdiv, seams)[1]
        out_u = [t - l - (q - d) for t, l, q, d in zip(u, lap_su, below, sdiv)]
        out_v = [
            t - l - (jnp.where(self.first, 0.0, pltpu.roll(d, 1, 1)) - jnp.where(self.last, 0.0, d))
            for t, l, d in zip(v, lap_sv, sdiv)
        ]
        return out_u, out_v

    def turn(self, x, by):
        return x if by % 8 == 0 else pltpu.roll(x, by % 8, 0)

    def ends(self, first, last, high, low):
        return [
            jnp.where(self.row < 6, self.turn(last, 6), high),
            jnp.where(self.row < 2, low, self.turn(first, 2)),
        ]


def kernel(
    sizes,
    obsm, obsv, cell, perm, mult_h, inc_h, err_h, div_h, bih_h, w_h,
    model, obs_o, state,
    mult, inc, err, div, bih, w, prev,
    adj_in, adj_ed, bwd_in, bwd_ed, mid_a, mid_f,
    up_s, down_s, low_r, high_r, four_s, four_r, perm_s, perm_r,
    a_hi, a_lo, wide, hot,
    load_sem, send_sem, recv_sem, store_sem, note_sem,
):
    levels, rows, cols, count, n_tm, n_patch = sizes
    per = levels // CHUNKS
    k, p = lax.axis_index("tm"), lax.axis_index("patch")
    k_next, k_prev = lax.rem(k + 1, n_tm), lax.rem(k + n_tm - 1, n_tm)
    p_next, p_prev = lax.rem(p + 1, n_patch), lax.rem(p + n_patch - 1, n_patch)
    has_next, has_prev = k < n_tm - 1, k > 0
    quad = lax.rem(p, 4)
    early, late = quad < 2, quad >= 2

    loads = [
        pltpu.make_async_copy(src, dst, load_sem.at[i])
        for i, (src, dst) in enumerate(
            ((mult_h, mult), (div_h, div), (bih_h, bih), (inc_h, inc), (w_h, w), (err_h, err))
        )
    ]
    for load in loads[:3]:
        load.start()

    def remote(index, src, dst, peer):
        return pltpu.make_async_remote_copy(
            src_ref=src, dst_ref=dst, send_sem=send_sem.at[index], recv_sem=recv_sem.at[index],
            device_id=peer, device_id_type=MESH,
        )

    def note(index, peer):
        pl.semaphore_signal(note_sem.at[index], inc=1, device_id=peer, device_id_type=MESH)

    RIM_UP, RIM_DOWN, BACK_IN, BACK_ED, BULK, INC_UP, INC_DOWN, ADJ_UP, ADJ_DOWN, FWD_UP, FWD_DOWN, PERM = (
        i * CHUNKS for i in range(12)
    )
    BULK_ENDS = PERM + 1
    FROM_ABOVE, FROM_BELOW, BESIDE_ABOVE, BESIDE_BELOW = range(4)

    def rim_up(c):
        return remote(RIM_UP + c, up_s.at[c], low_r.at[c], (k, p_next))

    def rim_down(c):
        return remote(RIM_DOWN + c, down_s.at[c], high_r.at[c], (k, p_prev))

    def back_in(c):
        span = pl.ds(c * per, per)
        return remote(BACK_IN + c, adj_in.at[:, span], bwd_in.at[:, span], (k_prev, p))

    def back_ed(c):
        span = pl.ds(c * per, per)
        return remote(BACK_ED + c, adj_ed.at[:, span], bwd_ed.at[:, span], (k_prev, p))

    send_perm = remote(PERM, perm_s, perm_r, (k, p_prev))

    def bulk(c):
        part = (slice(None), pl.ds(c * per, per), pl.ds(8, rows - 16))
        return remote(BULK + c, inc_h.at[part], prev.at[part], (k_next, p))

    def bulk_end(i):
        part = (slice(None), slice(None), pl.ds(i * (rows - 8), 8))
        return remote(BULK_ENDS + i, inc_h.at[part], prev.at[part], (k_next, p))

    def inc_up(c):
        return remote(INC_UP + c, four_s.at[0, c], four_r.at[0, c], (k_next, p_next))

    def inc_down(c):
        return remote(INC_DOWN + c, four_s.at[1, c], four_r.at[1, c], (k_next, p_prev))

    def adj_up(c):
        return remote(ADJ_UP + c, four_s.at[2, c], four_r.at[2, c], (k, p_next))

    def adj_down(c):
        return remote(ADJ_DOWN + c, four_s.at[3, c], four_r.at[3, c], (k, p_prev))

    def fwd_up(c):
        return remote(FWD_UP + c, four_s.at[4, c], four_r.at[4, c], (k, p_next))

    def fwd_down(c):
        return remote(FWD_DOWN + c, four_s.at[5, c], four_r.at[5, c], (k, p_prev))

    def start_all(*copies):
        for copy in copies:
            for c in range(CHUNKS):
                copy(c).start()

    def start_next(*copies):
        @pl.when(has_next)
        def _():
            start_all(*copies)

    barrier = pltpu.get_barrier_semaphore()
    for peer in ((k_prev, p), (k_next, p)):
        pl.semaphore_signal(barrier, inc=1, device_id=peer, device_id_type=MESH)

    @pl.when(quad != 3)
    def _():
        pl.semaphore_signal(barrier, inc=1, device_id=(k, p_next), device_id_type=MESH)

    @pl.when(quad == 0)
    def _():
        pl.semaphore_signal(barrier, inc=1, device_id=(k, p_prev), device_id_type=MESH)

    pl.semaphore_wait(barrier, jnp.where(quad == 0, 2, jnp.where(quad == 3, 4, 3)))

    def send_inc_up():
        pl.semaphore_wait(note_sem.at[BESIDE_ABOVE], 1)
        start_next(inc_up)

    def send_inc_down():
        pl.semaphore_wait(note_sem.at[BESIDE_BELOW], 1)
        start_next(inc_down)

    @pl.when(quad != 0)
    def _():
        note(FROM_ABOVE, (k, p_prev))
        note(BESIDE_BELOW, (k_prev, p))

    @pl.when(quad == 3)
    def _():
        note(FROM_BELOW, (k, p_next))
        note(BESIDE_ABOVE, (k_prev, p))

    @pl.when(has_next)
    def _():
        bulk_end(0).start()
        bulk_end(1).start()

    @pl.when(early)
    def _():
        start_next(bulk)

    st = Stencil(cols)
    perm_s[...] = jnp.broadcast_to(perm[...], perm_s.shape)
    for load in loads[:3]:
        load.wait()
    for load in loads[3:]:
        load.start()

    def pack(c, _):
        span = pl.ds(c * per, per)
        for var in range(2):
            up_s[c, :, 2 * var : 2 * var + 2, :] = mult[var, span, rows - 2 :, :]
            down_s[c, :, 2 * var : 2 * var + 2, :] = mult[var, span, :2, :]
            up_s[c, :, 4 + var : 5 + var, :] = div[var, span, rows - 1 :, :]
            up_s[c, :, 6 + var : 7 + var, :] = bih[var, span, rows - 1 :, :]
            down_s[c, :, 4 + var : 5 + var, :] = bih[var, span, :1, :]
            down_s[c, :, 6 + var : 7 + var, :] = bih[var, span, :1, :]
        return 0

    lax.fori_loop(0, CHUNKS, pack, 0)

    def send_up():
        start_all(rim_up)

    def send_down():
        send_perm.start()
        start_all(rim_down)

    def meet_above():
        pl.semaphore_wait(note_sem.at[FROM_ABOVE], 1)
        send_up()
        note(BESIDE_ABOVE, (k_prev, p))

    @pl.when(quad != 0)
    def _():
        send_down()

    @pl.when(quad == 3)
    def _():
        send_up()

    @pl.when(quad == 2)
    def _():
        meet_above()

    loads[3].wait()

    def pack_inc(c, _):
        for g in range(per):
            for var in range(2):
                at = 4 * (g % 2) + 2 * var
                four_s[0, c, g // 2, at : at + 2, :] = inc[var, c * per + g, rows - 2 :, :]
                four_s[1, c, g // 2, at : at + 2, :] = inc[var, c * per + g, :2, :]
        return 0

    lax.fori_loop(0, CHUNKS, pack_inc, 0)

    @pl.when(quad != 0)
    def _():
        send_inc_down()

    @pl.when(late)
    def _():
        send_inc_up()

    def tiles(field, lev):
        return [field[lev, 8 * i : 8 * (i + 1), :] for i in range(rows // 8)]

    def inside(lev, field, mid, order):
        u, v = tiles(field.at[0], lev), tiles(field.at[1], lev)
        for at, s in enumerate(order):
            u, v = st.step(u, v, tiles(div.at[s], lev), tiles(bih.at[s], lev), ())
            if at == 0:
                for var, f in ((0, u), (1, v)):
                    mid[var, lev, 2:8, :] = f[0][2:]
                    for i in range(1, rows // 8 - 1):
                        mid[var, lev, 8 * i : 8 * (i + 1), :] = f[i]
                    mid[var, lev, rows - 8 : rows - 2, :] = f[-1][:6]
        return u, v

    def adjoint_inside(c, _):
        for g in range(per):
            lev = c * per + g
            for var, f in enumerate(inside(lev, mult, mid_a, (1, 0))):
                adj_in[var, lev, :4, :] = f[0][4:]
                for i in range(1, rows // 8 - 1):
                    adj_in[var, lev, 8 * i - 4 : 8 * i + 4, :] = f[i]
                adj_in[var, lev, rows - 12 :, :] = f[-1][:4]

        @pl.when(early & has_prev)
        def _():
            back_in(c).start()

        return 0

    lax.fori_loop(0, CHUNKS, adjoint_inside, 0)

    @pl.when(early)
    def _():
        meet_above()

    @pl.when(quad == 1)
    def _():
        send_inc_up()

    @pl.when(late)
    def _():
        start_next(bulk)

    for load in loads[4:]:
        load.wait()

    def observations():
        half = rows // 2
        cells = cell[...]
        row = cells // cols
        within = (row // half) * cols + cells % cols
        group = row % half
        hot[...] = (
            lax.broadcasted_iota(jnp.int32, (2 * cols, count), 0) == jnp.broadcast_to(within, (2 * cols, count))
        ).astype(jnp.float32).astype(jnp.bfloat16)
        mask = lax.broadcasted_iota(jnp.int32, (half, count), 0) == jnp.broadcast_to(group, (half, count))
        times = obsm[...]
        for var in range(2):
            for lev in range(levels):
                at = (var * levels + lev) * half
                weight = w[var * levels + lev : var * levels + lev + 1, :]
                hi, lo = split(jnp.where(mask, jnp.broadcast_to(weight * times, mask.shape), 0.0))
                a_hi[at : at + half] = hi
                a_lo[at : at + half] = lo
                plane = inc[var, lev]
                hi, lo = split(jnp.concatenate([plane[:half], plane[half:]], 1))
                wide[at : at + half, : 2 * cols] = hi
                wide[at : at + half, 2 * cols :] = lo
        block = min(256, count)
        for start in range(0, count, block):
            part = hot[:, start : start + block]
            found = dot_nn(wide[...], jnp.concatenate([part, part], 0))
            found = found.reshape(2 * levels, half, block)
            found = jnp.where(mask[None, :, start : start + block], found, 0.0)
            found = jnp.sum(found.reshape(2 * levels, half // 8, 8, block), 1)
            found = found * w[:, start : start + block][:, None, :]
            found = jnp.sum(jnp.sum(found, 0), 0, keepdims=True)
            span = pl.ds(start, block)
            obs_o[:, span] = obsv[:, span] * obsm[:, span] + found
        spread = dot_nt(a_hi[...], hot[...]) + dot_nt(a_lo[...], hot[...])
        spread = spread.reshape(2, levels, half, 2 * cols)
        state[:, :, :half, :] = mult[:, :, :half, :] + spread[..., :cols]
        state[:, :, half:, :] = mult[:, :, half:, :] + spread[..., cols:]

    @pl.when(early)
    def _():
        observations()

    @pl.when(quad == 0)
    def _():
        send_inc_up()
        pl.semaphore_wait(note_sem.at[FROM_BELOW], 1)
        send_down()
        note(BESIDE_BELOW, (k_prev, p))
        send_inc_down()

    def keep(var, lev, at, f):
        span = slice(at, at + f.shape[0])
        rest = err[var, lev, span, :] * mult[var, lev, span, :] + inc[var, lev, span, :]
        model[var, lev, span, :] = rest - jnp.where(has_prev, f, 0.0)

    def forward_inside(c, _):
        @pl.when(has_prev)
        def _():
            bulk(c).wait_recv()

        for g in range(per):
            lev = c * per + g
            for var, f in enumerate(inside(lev, prev, mid_f, (0, 1))):
                keep(var, lev, 4, f[0][4:])
                for i in range(1, rows // 8 - 1):
                    keep(var, lev, 8 * i, f[i])
                keep(var, lev, rows - 8, f[-1][:4])
        return 0

    def all_forward_inside():
        @pl.when(early & has_prev)
        def _():
            bulk_end(0).wait_recv()
            bulk_end(1).wait_recv()

        lax.fori_loop(0, CHUNKS, forward_inside, 0)

    @pl.when(early)
    def _():
        all_forward_inside()

    def outer(field, lev):
        return field[lev, :8, :], field[lev, rows - 8 :, :]

    def border(field, lev, high, low, at):
        return [
            st.ends(*outer(field.at[var], lev), st.turn(high, 6 - at - 2 * var), st.turn(low, -at - 2 * var))
            for var in range(2)
        ]

    def border_coefs(c, g, s):
        lev = c * per + g
        high, low = high_r[c, g], low_r[c, g]
        a, b = outer(div.at[s], lev), outer(bih.at[s], lev)
        return (
            st.ends(*a, st.turn(a[1], 6), st.turn(low, 1 - (4 + s))),
            st.ends(*b, st.turn(high, 6 - (4 + s)), st.turn(low, 1 - (6 + s))),
        )

    def first_step(c, g, field, high, low, at, s, mid, above_s, below_s):
        lev = c * per + g
        found = st.step(*border(field, lev, high, low, at), *border_coefs(c, g, s), seams)
        for var, f in enumerate(found):
            place = 4 * (g % 2) + 2 * var
            mid[var, lev, rows - 2 :, :] = f[0][4:6]
            mid[var, lev, :2, :] = f[1][2:4]
            above_s[c, g // 2, place : place + 2, :] = f[0][4:6]
            below_s[c, g // 2, place : place + 2, :] = f[1][2:4]

    def second_step(c, g, mid, high, low, s):
        lev = c * per + g
        return st.step(*border(mid, lev, high, low, 4 * (g % 2)), *border_coefs(c, g, s), seams)

    send_perm.wait_recv()
    own, above = perm_s[...], perm_r[...]

    def seam(i, perm_index):
        crossing = jnp.where(st.above_edge[i], inverse_rows(perm_index), st.lane)
        return jnp.where(st.below_edge[i], perm_index, crossing)

    seams = (seam(0, above), seam(1, own))

    def adjoint_first(c, _):
        rim_up(c).wait_recv()
        rim_down(c).wait_recv()
        for g in range(per):
            first_step(c, g, mult, high_r[c, g], low_r[c, g], 0, 1, mid_a, four_s.at[2], four_s.at[3])
        adj_up(c).start()
        adj_down(c).start()

        @pl.when(late & has_prev)
        def _():
            back_in(c).start()

        return 0

    lax.fori_loop(0, CHUNKS, adjoint_first, 0)

    @pl.when(late & has_prev)
    def _():
        bulk_end(0).wait_recv()
        bulk_end(1).wait_recv()

    def forward_first(c, _):
        @pl.when(has_prev)
        def _():
            inc_up(c).wait_recv()
            inc_down(c).wait_recv()
            for g in range(per):
                high, low = four_r[1, c, g // 2], four_r[0, c, g // 2]
                first_step(c, g, prev, high, low, 4 * (g % 2), 0, mid_f, four_s.at[4], four_s.at[5])
            fwd_up(c).start()
            fwd_down(c).start()

        return 0

    lax.fori_loop(0, CHUNKS, forward_first, 0)

    @pl.when(late)
    def _():
        observations()


    def adjoint_second(c, _):
        adj_up(c).wait_recv()
        adj_down(c).wait_recv()
        for g in range(per):
            found = second_step(c, g, mid_a, four_r[3, c, g // 2], four_r[2, c, g // 2], 0)
            for var, f in enumerate(found):
                adj_ed[var, c * per + g] = jnp.where(st.row < 4, st.turn(f[0], 6), st.turn(f[1], 2))

        @pl.when(has_prev)
        def _():
            back_ed(c).start()

        return 0

    lax.fori_loop(0, CHUNKS, adjoint_second, 0)

    @pl.when(late)
    def _():
        all_forward_inside()

    def forward_second(c, _):
        @pl.when(has_prev)
        def _():
            fwd_up(c).wait_recv()
            fwd_down(c).wait_recv()

        for g in range(per):
            found = second_step(c, g, mid_f, four_r[5, c, g // 2], four_r[4, c, g // 2], 1)
            for var, f in enumerate(found):
                keep(var, c * per + g, rows - 4, f[0][2:6])
                keep(var, c * per + g, 0, f[1][2:6])
        return 0

    lax.fori_loop(0, CHUNKS, forward_second, 0)

    def finish(c, _):
        span = pl.ds(c * per, per)

        @pl.when(has_next)
        def _():
            back_in(c).wait_recv()
            back_ed(c).wait_recv()

        for at, part in (
            (4, bwd_in[:, span]),
            (rows - 4, bwd_ed[:, span, :4, :]),
            (0, bwd_ed[:, span, 4:, :]),
        ):
            place = slice(at, at + part.shape[2])
            state[:, span, place, :] = state[:, span, place, :] - jnp.where(has_next, part, 0.0)
        return 0

    lax.fori_loop(0, CHUNKS, finish, 0)

    def sent(c, _):
        rim_up(c).wait_send()
        rim_down(c).wait_send()
        adj_up(c).wait_send()
        adj_down(c).wait_send()

        @pl.when(has_prev)
        def _():
            back_in(c).wait_send()
            back_ed(c).wait_send()
            fwd_up(c).wait_send()
            fwd_down(c).wait_send()

        @pl.when(has_next)
        def _():
            bulk(c).wait_send()

            @pl.when(c < 2)
            def _():
                bulk_end(c).wait_send()

            inc_up(c).wait_send()
            inc_down(c).wait_send()

        return 0

    lax.fori_loop(0, CHUNKS, sent, 0)
    send_perm.wait_send()


def hand_over(*refs):
    sems = refs[-1]
    copies = [pltpu.make_async_copy(refs[i], refs[3 + i], sems.at[i]) for i in range(3)]
    for copy in copies:
        copy.start()
    for copy in copies:
        copy.wait()


def solution(mesh):
    n_tm, n_patch = mesh.shape["tm"], mesh.shape["patch"]

    def per_device(mult, obsm, inc, err, obsv, div, bih, w, cell, perm):
        _, _, levels, rows, cols = mult.shape
        count = obsm.shape[1]
        per = levels // CHUNKS
        whole = (2, levels, rows, cols)
        eight, four = (CHUNKS, per, 8, cols), (6, CHUNKS, per // 2, 8, cols)
        f32 = functools.partial(pltpu.VMEM, dtype=jnp.float32)
        scratch = [f32(whole)] * 5 + [f32((2 * levels, count)), f32(whole)]
        scratch += [f32((2, levels, rows - 8, cols)), f32((2, levels, 8, cols))] * 2
        scratch += [f32(whole)] * 2 + [f32(eight)] * 4 + [f32(four)] * 2
        scratch += [pltpu.VMEM((8, cols), jnp.int32)] * 2
        tall = 2 * levels * (rows // 2)
        scratch += [
            pltpu.VMEM((tall, count), jnp.bfloat16),
            pltpu.VMEM((tall, count), jnp.bfloat16),
            pltpu.VMEM((tall, 4 * cols), jnp.bfloat16),
            pltpu.VMEM((2 * cols, count), jnp.bfloat16),
        ]
        copies = 11 * CHUNKS + 3
        scratch += [
            pltpu.SemaphoreType.DMA((6,)),
            pltpu.SemaphoreType.DMA((copies,)),
            pltpu.SemaphoreType.DMA((copies,)),
            pltpu.SemaphoreType.DMA((2 * CHUNKS,)),
            pltpu.SemaphoreType.REGULAR((4,)),
        ]
        vmem, any_ = pl.BlockSpec(memory_space=pltpu.VMEM), pl.BlockSpec(memory_space=pl.ANY)
        shapes = (
            jax.ShapeDtypeStruct(whole, jnp.float32),
            jax.ShapeDtypeStruct((1, count), jnp.float32),
            jax.ShapeDtypeStruct(whole, jnp.float32),
        )
        parts = pl.pallas_call(
            functools.partial(kernel, (levels, rows, cols, count, n_tm, n_patch)),
            out_shape=tuple(pltpu.VMEM(x.shape, x.dtype) for x in shapes),
            in_specs=[vmem] * 4 + [any_] * 6,
            out_specs=(vmem, vmem, vmem),
            scratch_shapes=scratch,
            compiler_params=pltpu.CompilerParams(
                collective_id=0, has_side_effects=True, vmem_limit_bytes=62914560
            ),
        )(
            obsm, obsv, cell, perm, mult.reshape(whole), inc.reshape(whole), err.reshape(whole),
            div.reshape(whole), bih.reshape(whole), w.reshape(2 * levels, count),
        )
        model, obs, state = pl.pallas_call(
            hand_over,
            out_shape=shapes,
            in_specs=[vmem] * 3,
            out_specs=(any_,) * 3,
            scratch_shapes=[pltpu.SemaphoreType.DMA((3,))],
            compiler_params=pltpu.CompilerParams(vmem_limit_bytes=16777216),
        )(*parts)
        return model[None], obs, state[None]

    field = P("tm", None, None, "patch", None)
    per_obs = P("tm", "patch")
    return jax.shard_map(
        per_device,
        mesh=mesh,
        in_specs=(
            field, per_obs, field, field, per_obs, field, field,
            P("tm", None, None, "patch"), per_obs, P("patch", None),
        ),
        out_specs=(field, per_obs, field),
        check_vma=False,
    )
```

```python
import functools

import jax
import jax.numpy as jnp
from jax import lax
from jax.experimental import pallas as pl
from jax.experimental.pallas import tpu as pltpu
from jax.sharding import PartitionSpec as P

MESH = pl.DeviceIdType.MESH
CHUNKS = 4


def dot_nt(a, b):
    return lax.dot_general(a, b, (((1,), (1,)), ((), ())), preferred_element_type=jnp.float32)


def dot_nn(a, b):
    return lax.dot_general(a, b, (((1,), (0,)), ((), ())), preferred_element_type=jnp.float32)


def split(x):
    hi = x.astype(jnp.bfloat16)
    return hi, (x - hi.astype(jnp.float32)).astype(jnp.bfloat16)


def inverse_rows(perm):
    cols = perm.shape[1]
    target = lax.broadcasted_iota(jnp.int32, (cols, cols), 0)
    hot = (jnp.broadcast_to(perm[0:1], (cols, cols)) == target).astype(jnp.float32).astype(jnp.bfloat16)
    source = lax.broadcasted_iota(jnp.int32, perm.shape, 1).astype(jnp.float32).astype(jnp.bfloat16)
    return dot_nt(source, hot).astype(jnp.int32)


def lane_take(tile, index):
    return jnp.take_along_axis(tile, index, axis=1, mode="promise_in_bounds")

class Stencil:
    def __init__(self, cols):
        self.cols = cols
        self.row = lax.broadcasted_iota(jnp.int32, (8, cols), 0)
        self.lane = lax.broadcasted_iota(jnp.int32, (8, cols), 1)
        self.first, self.last = self.lane == 0, self.lane == cols - 1
        self.top, self.bottom = self.row == 7, self.row == 0
        self.below_edge = (self.row == 5, self.row == 1)
        self.above_edge = (self.row == 6, self.row == 2)

    def up(self, tiles):
        r = [pltpu.roll(t, 7, 0) for t in tiles]
        return [jnp.where(self.top, r[(i + 1) % len(r)], r[i]) for i in range(len(r))]

    def down(self, tiles):
        r = [pltpu.roll(t, 1, 0) for t in tiles]
        return [jnp.where(self.bottom, r[i - 1], r[i]) for i in range(len(r))]

    def rows_around(self, tiles, seams):
        above, below = list(tiles), list(tiles)
        for i, index in enumerate(seams):
            crossed = lane_take(tiles[i], index)
            above[i] = jnp.where(self.above_edge[i], crossed, tiles[i])
            below[i] = jnp.where(self.below_edge[i], crossed, tiles[i])
        return self.up(above), self.down(below)

    def right(self, tiles):
        return [jnp.where(self.last, t, pltpu.roll(t, self.cols - 1, 1)) for t in tiles]

    def left(self, tiles):
        return [jnp.where(self.first, t, pltpu.roll(t, 1, 1)) for t in tiles]

    def lap(self, f, above, below, right):
        return [(a + b) + (r + l) - 4.0 * t for t, a, b, r, l in zip(f, above, below, right, self.left(f))]

    def step(self, u, v, a, b, seams):
        up_u, down_u = self.rows_around(u, seams)
        up_v, down_v = self.rows_around(v, seams)
        right_v = self.right(v)
        sdiv = [c * ((q - p) + (s - r)) for c, p, q, r, s in zip(a, u, up_u, v, right_v)]
        su = [c * t for c, t in zip(b, self.lap(u, up_u, down_u, self.right(u)))]
        sv = [c * t for c, t in zip(b, self.lap(v, up_v, down_v, right_v))]
        lap_su = self.lap(su, *self.rows_around(su, seams), self.right(su))
        lap_sv = self.lap(sv, *self.rows_around(sv, seams), self.right(sv))
        below = self.rows_around(sdiv, seams)[1]
        out_u = [t - l - (q - d) for t, l, q, d in zip(u, lap_su, below, sdiv)]
        out_v = [
            t - l - (jnp.where(self.first, 0.0, pltpu.roll(d, 1, 1)) - jnp.where(self.last, 0.0, d))
            for t, l, d in zip(v, lap_sv, sdiv)
        ]
        return out_u, out_v

    def turn(self, x, by):
        return x if by % 8 == 0 else pltpu.roll(x, by % 8, 0)

    def ends(self, first, last, high, low):
        return [
            jnp.where(self.row < 6, self.turn(last, 6), high),
            jnp.where(self.row < 2, low, self.turn(first, 2)),
        ]


def kernel(
    sizes,
    obsm, obsv, cell, perm, mult_h, inc_h, err_h, div_h, bih_h, w_h,
    model, obs_o, state,
    mult, inc, err, div, bih, w, prev,
    adj_in, adj_ed, bwd_in, bwd_ed, mid_a, mid_f,
    up_s, down_s, low_r, high_r, four_s, four_r, perm_s, perm_r,
    a_hi, a_lo, wide, hot,
    load_sem, send_sem, recv_sem, store_sem, note_sem,
):
    levels, rows, cols, count, n_tm, n_patch = sizes
    per = levels // CHUNKS
    k, p = lax.axis_index("tm"), lax.axis_index("patch")
    k_next, k_prev = lax.rem(k + 1, n_tm), lax.rem(k + n_tm - 1, n_tm)
    p_next, p_prev = lax.rem(p + 1, n_patch), lax.rem(p + n_patch - 1, n_patch)
    has_next, has_prev = k < n_tm - 1, k > 0
    quad = lax.rem(p, 4)
    early, late = quad < 2, quad >= 2
    inside_first, inside_last = quad == 0, quad != 0

    loads = [
        pltpu.make_async_copy(src, dst, load_sem.at[i])
        for i, (src, dst) in enumerate(
            ((mult_h, mult), (div_h, div), (bih_h, bih), (inc_h, inc), (w_h, w), (err_h, err))
        )
    ]
    for load in loads[:3]:
        load.start()

    def remote(index, src, dst, peer):
        return pltpu.make_async_remote_copy(
            src_ref=src, dst_ref=dst, send_sem=send_sem.at[index], recv_sem=recv_sem.at[index],
            device_id=peer, device_id_type=MESH,
        )

    def note(index, peer):
        pl.semaphore_signal(note_sem.at[index], inc=1, device_id=peer, device_id_type=MESH)

    RIM_UP, RIM_DOWN, BACK_IN, BACK_ED, BULK, INC_UP, INC_DOWN, ADJ_UP, ADJ_DOWN, FWD_UP, FWD_DOWN, PERM = (
        i * CHUNKS for i in range(12)
    )
    BULK_ENDS = PERM + 1
    FROM_ABOVE, FROM_BELOW, BESIDE_ABOVE, BESIDE_BELOW = range(4)

    def rim_up(c):
        return remote(RIM_UP + c, up_s.at[c], low_r.at[c], (k, p_next))

    def rim_down(c):
        return remote(RIM_DOWN + c, down_s.at[c], high_r.at[c], (k, p_prev))

    def back_in(c):
        span = pl.ds(c * per, per)
        return remote(BACK_IN + c, adj_in.at[:, span], bwd_in.at[:, span], (k_prev, p))

    def back_ed(c):
        span = pl.ds(c * per, per)
        return remote(BACK_ED + c, adj_ed.at[:, span], bwd_ed.at[:, span], (k_prev, p))

    send_perm = remote(PERM, perm_s, perm_r, (k, p_prev))

    def bulk(c):
        part = (slice(None), pl.ds(c * per, per), pl.ds(8, rows - 16))
        return remote(BULK + c, inc_h.at[part], prev.at[part], (k_next, p))

    def bulk_end(i):
        part = (slice(None), slice(None), pl.ds(i * (rows - 8), 8))
        return remote(BULK_ENDS + i, inc_h.at[part], prev.at[part], (k_next, p))

    def inc_up(c):
        return remote(INC_UP + c, four_s.at[0, c], four_r.at[0, c], (k_next, p_next))

    def inc_down(c):
        return remote(INC_DOWN + c, four_s.at[1, c], four_r.at[1, c], (k_next, p_prev))

    def adj_up(c):
        return remote(ADJ_UP + c, four_s.at[2, c], four_r.at[2, c], (k, p_next))

    def adj_down(c):
        return remote(ADJ_DOWN + c, four_s.at[3, c], four_r.at[3, c], (k, p_prev))

    def fwd_up(c):
        return remote(FWD_UP + c, four_s.at[4, c], four_r.at[4, c], (k, p_next))

    def fwd_down(c):
        return remote(FWD_DOWN + c, four_s.at[5, c], four_r.at[5, c], (k, p_prev))

    def start_all(*copies):
        for copy in copies:
            for c in range(CHUNKS):
                copy(c).start()

    def start_next(*copies):
        @pl.when(has_next)
        def _():
            start_all(*copies)

    barrier = pltpu.get_barrier_semaphore()
    for peer in ((k_prev, p), (k_next, p)):
        pl.semaphore_signal(barrier, inc=1, device_id=peer, device_id_type=MESH)

    @pl.when(quad != 3)
    def _():
        pl.semaphore_signal(barrier, inc=1, device_id=(k, p_next), device_id_type=MESH)

    @pl.when(quad == 0)
    def _():
        pl.semaphore_signal(barrier, inc=1, device_id=(k, p_prev), device_id_type=MESH)

    pl.semaphore_wait(barrier, jnp.where(quad == 0, 2, jnp.where(quad == 3, 4, 3)))

    def send_inc_up():
        pl.semaphore_wait(note_sem.at[BESIDE_ABOVE], 1)
        start_next(inc_up)

    def send_inc_down():
        pl.semaphore_wait(note_sem.at[BESIDE_BELOW], 1)
        start_next(inc_down)

    @pl.when(quad != 0)
    def _():
        note(FROM_ABOVE, (k, p_prev))
        note(BESIDE_BELOW, (k_prev, p))

    @pl.when(quad == 3)
    def _():
        note(FROM_BELOW, (k, p_next))
        note(BESIDE_ABOVE, (k_prev, p))

    @pl.when(has_next)
    def _():
        bulk_end(0).start()
        bulk_end(1).start()

    @pl.when(early)
    def _():
        start_next(bulk)

    st = Stencil(cols)
    perm_s[...] = jnp.broadcast_to(perm[...], perm_s.shape)
    for load in loads[:3]:
        load.wait()
    for load in loads[3:]:
        load.start()

    def pack(c, _):
        span = pl.ds(c * per, per)
        for var in range(2):
            up_s[c, :, 2 * var : 2 * var + 2, :] = mult[var, span, rows - 2 :, :]
            down_s[c, :, 2 * var : 2 * var + 2, :] = mult[var, span, :2, :]
            up_s[c, :, 4 + var : 5 + var, :] = div[var, span, rows - 1 :, :]
            up_s[c, :, 6 + var : 7 + var, :] = bih[var, span, rows - 1 :, :]
            down_s[c, :, 4 + var : 5 + var, :] = bih[var, span, :1, :]
            down_s[c, :, 6 + var : 7 + var, :] = bih[var, span, :1, :]
        return 0

    lax.fori_loop(0, CHUNKS, pack, 0)

    def send_up():
        start_all(rim_up)

    def send_down():
        send_perm.start()
        start_all(rim_down)

    def meet_above():
        pl.semaphore_wait(note_sem.at[FROM_ABOVE], 1)
        send_up()
        note(BESIDE_ABOVE, (k_prev, p))

    @pl.when(quad == 3)
    def _():
        send_up()

    @pl.when(quad != 0)
    def _():
        send_down()

    @pl.when(quad == 2)
    def _():
        meet_above()

    loads[3].wait()

    def pack_inc(c, _):
        for g in range(per):
            for var in range(2):
                at = 4 * (g % 2) + 2 * var
                four_s[0, c, g // 2, at : at + 2, :] = inc[var, c * per + g, rows - 2 :, :]
                four_s[1, c, g // 2, at : at + 2, :] = inc[var, c * per + g, :2, :]
        return 0

    lax.fori_loop(0, CHUNKS, pack_inc, 0)

    @pl.when(late)
    def _():
        send_inc_up()

    @pl.when(quad != 0)
    def _():
        send_inc_down()

    def tiles(field, lev):
        return [field[lev, 8 * i : 8 * (i + 1), :] for i in range(rows // 8)]

    def inside(lev, field, mid, order):
        u, v = tiles(field.at[0], lev), tiles(field.at[1], lev)
        for at, s in enumerate(order):
            u, v = st.step(u, v, tiles(div.at[s], lev), tiles(bih.at[s], lev), ())
            if at == 0:
                for var, f in ((0, u), (1, v)):
                    mid[var, lev, 2:8, :] = f[0][2:]
                    for i in range(1, rows // 8 - 1):
                        mid[var, lev, 8 * i : 8 * (i + 1), :] = f[i]
                    mid[var, lev, rows - 8 : rows - 2, :] = f[-1][:6]
        return u, v

    def adjoint_inside(c, _):
        for g in range(per):
            lev = c * per + g
            for var, f in enumerate(inside(lev, mult, mid_a, (1, 0))):
                adj_in[var, lev, :4, :] = f[0][4:]
                for i in range(1, rows // 8 - 1):
                    adj_in[var, lev, 8 * i - 4 : 8 * i + 4, :] = f[i]
                adj_in[var, lev, rows - 12 :, :] = f[-1][:4]

        @pl.when((quad == 0) & has_prev)
        def _():
            back_in(c).start()

        return 0

    lax.fori_loop(0, CHUNKS, adjoint_inside, 0)

    @pl.when(early)
    def _():
        meet_above()

    @pl.when(quad == 1)
    def _():
        send_inc_up()

    @pl.when(late)
    def _():
        start_next(bulk)

    for load in loads[4:]:
        load.wait()

    def observations():
        half = rows // 2
        cells = cell[...]
        row = cells // cols
        within = (row // half) * cols + cells % cols
        group = row % half
        hot[...] = (
            lax.broadcasted_iota(jnp.int32, (2 * cols, count), 0) == jnp.broadcast_to(within, (2 * cols, count))
        ).astype(jnp.float32).astype(jnp.bfloat16)
        mask = lax.broadcasted_iota(jnp.int32, (half, count), 0) == jnp.broadcast_to(group, (half, count))
        times = obsm[...]
        for var in range(2):
            for lev in range(levels):
                at = (var * levels + lev) * half
                weight = w[var * levels + lev : var * levels + lev + 1, :]
                hi, lo = split(jnp.where(mask, jnp.broadcast_to(weight * times, mask.shape), 0.0))
                a_hi[at : at + half] = hi
                a_lo[at : at + half] = lo
                plane = inc[var, lev]
                hi, lo = split(jnp.concatenate([plane[:half], plane[half:]], 1))
                wide[at : at + half, : 2 * cols] = hi
                wide[at : at + half, 2 * cols :] = lo
        block = min(256, count)
        for start in range(0, count, block):
            part = hot[:, start : start + block]
            found = dot_nn(wide[...], jnp.concatenate([part, part], 0))
            found = found.reshape(2 * levels, half, block)
            found = jnp.where(mask[None, :, start : start + block], found, 0.0)
            found = jnp.sum(found.reshape(2 * levels, half // 8, 8, block), 1)
            found = found * w[:, start : start + block][:, None, :]
            found = jnp.sum(jnp.sum(found, 0), 0, keepdims=True)
            span = pl.ds(start, block)
            obs_o[:, span] = obsv[:, span] * obsm[:, span] + found
        spread = dot_nt(a_hi[...], hot[...]) + dot_nt(a_lo[...], hot[...])
        spread = spread.reshape(2, levels, half, 2 * cols)
        state[:, :, :half, :] = mult[:, :, :half, :] + spread[..., :cols]
        state[:, :, half:, :] = mult[:, :, half:, :] + spread[..., cols:]

    @pl.when(early)
    def _():
        observations()

    @pl.when(quad == 0)
    def _():
        send_inc_up()
        pl.semaphore_wait(note_sem.at[FROM_BELOW], 1)
        send_down()
        note(BESIDE_BELOW, (k_prev, p))
        send_inc_down()

    def keep(var, lev, at, f):
        span = slice(at, at + f.shape[0])
        rest = err[var, lev, span, :] * mult[var, lev, span, :] + inc[var, lev, span, :]
        model[var, lev, span, :] = rest - jnp.where(has_prev, f, 0.0)

    def forward_inside(c, _):
        @pl.when(has_prev)
        def _():
            bulk(c).wait_recv()

        for g in range(per):
            lev = c * per + g
            for var, f in enumerate(inside(lev, prev, mid_f, (0, 1))):
                keep(var, lev, 4, f[0][4:])
                for i in range(1, rows // 8 - 1):
                    keep(var, lev, 8 * i, f[i])
                keep(var, lev, rows - 8, f[-1][:4])
        return 0

    def all_forward_inside():
        @pl.when(inside_first & has_prev)
        def _():
            bulk_end(0).wait_recv()
            bulk_end(1).wait_recv()

        lax.fori_loop(0, CHUNKS, forward_inside, 0)

    @pl.when(inside_first)
    def _():
        all_forward_inside()

    def outer(field, lev):
        return field[lev, :8, :], field[lev, rows - 8 :, :]

    def border(field, lev, high, low, at):
        return [
            st.ends(*outer(field.at[var], lev), st.turn(high, 6 - at - 2 * var), st.turn(low, -at - 2 * var))
            for var in range(2)
        ]

    def border_coefs(c, g, s):
        lev = c * per + g
        high, low = high_r[c, g], low_r[c, g]
        a, b = outer(div.at[s], lev), outer(bih.at[s], lev)
        return (
            st.ends(*a, st.turn(a[1], 6), st.turn(low, 1 - (4 + s))),
            st.ends(*b, st.turn(high, 6 - (4 + s)), st.turn(low, 1 - (6 + s))),
        )

    def first_step(c, g, field, high, low, at, s, mid, above_s, below_s):
        lev = c * per + g
        found = st.step(*border(field, lev, high, low, at), *border_coefs(c, g, s), seams)
        for var, f in enumerate(found):
            place = 4 * (g % 2) + 2 * var
            mid[var, lev, rows - 2 :, :] = f[0][4:6]
            mid[var, lev, :2, :] = f[1][2:4]
            above_s[c, g // 2, place : place + 2, :] = f[0][4:6]
            below_s[c, g // 2, place : place + 2, :] = f[1][2:4]

    def second_step(c, g, mid, high, low, s):
        lev = c * per + g
        return st.step(*border(mid, lev, high, low, 4 * (g % 2)), *border_coefs(c, g, s), seams)

    send_perm.wait_recv()
    own, above = perm_s[...], perm_r[...]

    def seam(i, perm_index):
        crossing = jnp.where(st.above_edge[i], inverse_rows(perm_index), st.lane)
        return jnp.where(st.below_edge[i], perm_index, crossing)

    seams = (seam(0, above), seam(1, own))

    def adjoint_first(c, _):
        rim_up(c).wait_recv()
        rim_down(c).wait_recv()
        for g in range(per):
            first_step(c, g, mult, high_r[c, g], low_r[c, g], 0, 1, mid_a, four_s.at[2], four_s.at[3])
        adj_up(c).start()
        adj_down(c).start()

        @pl.when((quad != 0) & has_prev)
        def _():
            back_in(c).start()

        return 0

    lax.fori_loop(0, CHUNKS, adjoint_first, 0)

    @pl.when(inside_last & has_prev)
    def _():
        bulk_end(0).wait_recv()
        bulk_end(1).wait_recv()

    def forward_first(c, _):
        @pl.when(has_prev)
        def _():
            inc_up(c).wait_recv()
            inc_down(c).wait_recv()
            for g in range(per):
                high, low = four_r[1, c, g // 2], four_r[0, c, g // 2]
                first_step(c, g, prev, high, low, 4 * (g % 2), 0, mid_f, four_s.at[4], four_s.at[5])
            fwd_up(c).start()
            fwd_down(c).start()

        return 0

    lax.fori_loop(0, CHUNKS, forward_first, 0)

    @pl.when(late)
    def _():
        observations()


    def adjoint_second(c, _):
        adj_up(c).wait_recv()
        adj_down(c).wait_recv()
        for g in range(per):
            found = second_step(c, g, mid_a, four_r[3, c, g // 2], four_r[2, c, g // 2], 0)
            for var, f in enumerate(found):
                adj_ed[var, c * per + g] = jnp.where(st.row < 4, st.turn(f[0], 6), st.turn(f[1], 2))

        @pl.when(has_prev)
        def _():
            back_ed(c).start()

        return 0

    lax.fori_loop(0, CHUNKS, adjoint_second, 0)

    @pl.when(inside_last)
    def _():
        all_forward_inside()

    def forward_second(c, _):
        @pl.when(has_prev)
        def _():
            fwd_up(c).wait_recv()
            fwd_down(c).wait_recv()

        for g in range(per):
            found = second_step(c, g, mid_f, four_r[5, c, g // 2], four_r[4, c, g // 2], 1)
            for var, f in enumerate(found):
                keep(var, c * per + g, rows - 4, f[0][2:6])
                keep(var, c * per + g, 0, f[1][2:6])
        return 0

    lax.fori_loop(0, CHUNKS, forward_second, 0)

    def finish(c, _):
        span = pl.ds(c * per, per)

        @pl.when(has_next)
        def _():
            back_in(c).wait_recv()
            back_ed(c).wait_recv()

        for at, part in (
            (4, bwd_in[:, span]),
            (rows - 4, bwd_ed[:, span, :4, :]),
            (0, bwd_ed[:, span, 4:, :]),
        ):
            place = slice(at, at + part.shape[2])
            state[:, span, place, :] = state[:, span, place, :] - jnp.where(has_next, part, 0.0)
        return 0

    lax.fori_loop(0, CHUNKS, finish, 0)

    def sent(c, _):
        rim_up(c).wait_send()
        rim_down(c).wait_send()
        adj_up(c).wait_send()
        adj_down(c).wait_send()

        @pl.when(has_prev)
        def _():
            back_in(c).wait_send()
            back_ed(c).wait_send()
            fwd_up(c).wait_send()
            fwd_down(c).wait_send()

        @pl.when(has_next)
        def _():
            bulk(c).wait_send()

            @pl.when(c < 2)
            def _():
                bulk_end(c).wait_send()

            inc_up(c).wait_send()
            inc_down(c).wait_send()

        return 0

    lax.fori_loop(0, CHUNKS, sent, 0)
    send_perm.wait_send()


def hand_over(*refs):
    sems = refs[-1]
    copies = [pltpu.make_async_copy(refs[i], refs[3 + i], sems.at[i]) for i in range(3)]
    for copy in copies:
        copy.start()
    for copy in copies:
        copy.wait()


def solution(mesh):
    n_tm, n_patch = mesh.shape["tm"], mesh.shape["patch"]

    def per_device(mult, obsm, inc, err, obsv, div, bih, w, cell, perm):
        _, _, levels, rows, cols = mult.shape
        count = obsm.shape[1]
        per = levels // CHUNKS
        whole = (2, levels, rows, cols)
        eight, four = (CHUNKS, per, 8, cols), (6, CHUNKS, per // 2, 8, cols)
        f32 = functools.partial(pltpu.VMEM, dtype=jnp.float32)
        scratch = [f32(whole)] * 5 + [f32((2 * levels, count)), f32(whole)]
        scratch += [f32((2, levels, rows - 8, cols)), f32((2, levels, 8, cols))] * 2
        scratch += [f32(whole)] * 2 + [f32(eight)] * 4 + [f32(four)] * 2
        scratch += [pltpu.VMEM((8, cols), jnp.int32)] * 2
        tall = 2 * levels * (rows // 2)
        scratch += [
            pltpu.VMEM((tall, count), jnp.bfloat16),
            pltpu.VMEM((tall, count), jnp.bfloat16),
            pltpu.VMEM((tall, 4 * cols), jnp.bfloat16),
            pltpu.VMEM((2 * cols, count), jnp.bfloat16),
        ]
        copies = 11 * CHUNKS + 3
        scratch += [
            pltpu.SemaphoreType.DMA((6,)),
            pltpu.SemaphoreType.DMA((copies,)),
            pltpu.SemaphoreType.DMA((copies,)),
            pltpu.SemaphoreType.DMA((2 * CHUNKS,)),
            pltpu.SemaphoreType.REGULAR((4,)),
        ]
        vmem, any_ = pl.BlockSpec(memory_space=pltpu.VMEM), pl.BlockSpec(memory_space=pl.ANY)
        shapes = (
            jax.ShapeDtypeStruct(whole, jnp.float32),
            jax.ShapeDtypeStruct((1, count), jnp.float32),
            jax.ShapeDtypeStruct(whole, jnp.float32),
        )
        parts = pl.pallas_call(
            functools.partial(kernel, (levels, rows, cols, count, n_tm, n_patch)),
            out_shape=tuple(pltpu.VMEM(x.shape, x.dtype) for x in shapes),
            in_specs=[vmem] * 4 + [any_] * 6,
            out_specs=(vmem, vmem, vmem),
            scratch_shapes=scratch,
            compiler_params=pltpu.CompilerParams(
                collective_id=0, has_side_effects=True, vmem_limit_bytes=62914560
            ),
        )(
            obsm, obsv, cell, perm, mult.reshape(whole), inc.reshape(whole), err.reshape(whole),
            div.reshape(whole), bih.reshape(whole), w.reshape(2 * levels, count),
        )
        model, obs, state = pl.pallas_call(
            hand_over,
            out_shape=shapes,
            in_specs=[vmem] * 3,
            out_specs=(any_,) * 3,
            scratch_shapes=[pltpu.SemaphoreType.DMA((3,))],
            compiler_params=pltpu.CompilerParams(vmem_limit_bytes=16777216),
        )(*parts)
        return model[None], obs, state[None]

    field = P("tm", None, None, "patch", None)
    per_obs = P("tm", "patch")
    return jax.shard_map(
        per_device,
        mesh=mesh,
        in_specs=(
            field, per_obs, field, field, per_obs, field, field,
            P("tm", None, None, "patch"), per_obs, P("patch", None),
        ),
        out_specs=(field, per_obs, field),
        check_vma=False,
    )
```
